512 devices in a mesh: seq: 64 (over x, z), kvh: 8 (over y, core).
Axes of the slice: x: 4, y: 4, z: 16, core: 2. Of those that a mesh axis runs over, the one named last changes fastest.
Arguments:
- query_in: bfloat16 [16384, 8192], P(('seq', 'kvh')), may hold values from -8 to 8
- key_in: bfloat16 [16384, 1024], P(('seq', 'kvh')), may hold values from -8 to 8
- value_in: bfloat16 [16384, 1024], P(('seq', 'kvh')), may hold values from -6 to 6
- grad_out: bfloat16 [16384, 8192], P('seq', 'kvh'), may hold values from -6 to 6
- doc_lengths: int32 [64], replicated, may hold values from 1 to 769, 16384 in all
Outputs:
- attn_out: bfloat16 [16384, 8192], P('seq', 'kvh')
- grad_query: bfloat16 [16384, 8192], P('seq', 'kvh')
- grad_key: bfloat16 [16384, 1024], P('seq', 'kvh')
- grad_value: bfloat16 [16384, 1024], P('seq', 'kvh')
The draws below stay inside these ranges and needn't reach their ends.
Inputs may be any that keep to these rules, and one draw needn't show every extreme that they name: `doc_lengths`: the lengths sum to 16384; the longest document has exactly 769 tokens.
All inputs are finite; a program needn't handle non-finite values.
Results may differ from the reference program's by a relative error of at most 0.03.
Values may be sent and summed in bfloat16 or wider, within the bound.
A program may use at most 64 MiB of HBM per device.

```python
import math
import jax
import jax.numpy as jnp
import numpy as np
from jax import lax

HEADS = 64
KV_HEADS = 8
HEAD_DIM = 128
T_DEV = 256
SPAN = 3
TOKENS = 16384
DOCS = 64
MAXDOC = 769


def draw_query_in(key, part):
    key = jax.random.fold_in(key, 5)
    result = jnp.clip(jax.random.normal(key, (TOKENS, HEADS * HEAD_DIM), jnp.float32), -6.0, 6.0)
    return result.astype(jnp.bfloat16)


def draw_key_in(key, part):
    key = jax.random.fold_in(key, 9)
    result = jnp.clip(jax.random.normal(key, (TOKENS, KV_HEADS * HEAD_DIM), jnp.float32), -6.0, 6.0)
    return result.astype(jnp.bfloat16)


def levels(stream_key, dims, cuts, low, high):
    level = 1.0
    for position, parts in cuts:
        steps = jax.random.uniform(jax.random.fold_in(jax.random.fold_in(stream_key, 6), position), (parts,), jnp.float32, low / len(cuts), high / len(cuts))
        level = level * jnp.repeat(jnp.exp(steps), dims[position] // parts).reshape((-1,) + (1,) * (len(dims) - 1 - position))
    return level


def length_profile(count, total, limit, slope):
    weights = [(1 << 20) // math.isqrt(rank ** slope) + 1 for rank in range(2, count + 1)]
    spare, counts = total - limit - (count - 1), [1] * (count - 1)
    while spare > 0:
        free = [i for i in range(count - 1) if counts[i] < limit]
        mass, budget = sum([weights[i] for i in free]), spare
        for i in free:
            more = min(limit - counts[i], max(1, budget * weights[i] // mass), spare)
            counts[i] = counts[i] + more
            spare = spare - more
    return np.array([limit] + counts)


def uneven_parts(rng, amount, total, limit, skew):
    if amount == 2:
        one = jax.random.randint(rng, (), max(1, total - limit), min(limit, total - 1) + 1)
        return jnp.stack([one, total - one])
    lengths = jnp.asarray(length_profile(amount, total, limit, skew), jnp.int32)
    pairs = (amount - 1) // 2
    donor, taker = lengths[1:1 + 2 * pairs:2], lengths[2:2 + 2 * pairs:2]
    slack = jnp.minimum(donor - 1, limit - taker)
    moved = jax.random.randint(jax.random.fold_in(rng, 1), (pairs,), 0, 1 << 20) % (slack + 1)
    lengths = lengths.at[1:1 + 2 * pairs:2].set(donor - moved).at[2:2 + 2 * pairs:2].set(taker + moved)
    return lengths[jax.random.permutation(jax.random.fold_in(rng, 2), amount)]


def bell_draw(own_key, dims, width, most, pieces=(), held_as=jnp.bfloat16):
    values = width * jax.random.normal(own_key, dims, jnp.float32)
    if pieces:
        values = values * levels(own_key, dims, pieces, -0.22, 0.18)
    return jnp.clip(values, -most, most).astype(held_as)


def setup_inputs(seed: int = 0) -> dict:
    arg_keys = jax.random.split(jax.random.key(seed), 6)
    return {
        "query_in": draw_query_in(jax.random.fold_in(arg_keys[5], 71), 0),
        "key_in": draw_key_in(jax.random.fold_in(arg_keys[5], 71), 0),
        "value_in": bell_draw(arg_keys[2], (TOKENS, KV_HEADS * HEAD_DIM), 1.0, 6.0, ((0, 512),)),
        "grad_out": bell_draw(arg_keys[3], (TOKENS, HEADS * HEAD_DIM), 1.0, 6.0, ((0, 64), (1, 8))),
        "doc_lengths": uneven_parts(arg_keys[4], DOCS, TOKENS, MAXDOC, 2).astype(jnp.int32),
    }


def doc_index(positions, doc_lengths):
    doc_ends = jnp.cumsum(doc_lengths).astype(jnp.int32)
    return lax.optimization_barrier(jnp.sum((doc_ends[None, :] <= positions[:, None]).astype(jnp.int32), axis=1))

def window_mask(query_pos, key_pos, doc_lengths):
    query_doc = doc_index(query_pos, doc_lengths)
    key_doc = doc_index(key_pos, doc_lengths)
    return (key_pos[None, :] >= 0) & (key_pos[None, :] <= query_pos[:, None]) & (key_doc[None, :] == query_doc[:, None])

def head_pass(queries, key_win, value_win, grad_rows, visible, score_scale):
    scores = jnp.dot(queries, key_win.T, preferred_element_type=jnp.float32) * score_scale
    masked = jnp.where(visible, scores, -jnp.inf)
    row_max = lax.optimization_barrier(jnp.max(masked, axis=1, keepdims=True))
    shifted_exp = jnp.exp(masked - row_max)
    prob_f32 = shifted_exp / lax.optimization_barrier(jnp.sum(shifted_exp, axis=1, keepdims=True))
    prob_b = prob_f32.astype(jnp.bfloat16)
    attn_rows = jnp.dot(prob_b, value_win, preferred_element_type=jnp.float32).astype(jnp.bfloat16)
    row_delta = lax.optimization_barrier(jnp.sum(grad_rows.astype(jnp.float32) * attn_rows.astype(jnp.float32), axis=1, keepdims=True))
    part_dv = jnp.dot(prob_b.T, grad_rows, preferred_element_type=jnp.float32)
    grad_prob = jnp.dot(grad_rows, value_win.T, preferred_element_type=jnp.float32)
    grad_score = (prob_f32 * (grad_prob - row_delta) * score_scale).astype(jnp.bfloat16)
    grad_rows_q = jnp.dot(grad_score, key_win, preferred_element_type=jnp.float32).astype(jnp.bfloat16)
    part_dk = jnp.dot(grad_score.T, queries, preferred_element_type=jnp.float32)
    return (attn_rows, grad_rows_q, part_dk, part_dv)

def reference(query_in, key_in, value_in, grad_out, doc_lengths):
    group_size = HEADS // KV_HEADS
    win_blocks = SPAN + 1
    score_scale = 1.0 / math.sqrt(HEAD_DIM)
    num_blocks = TOKENS // T_DEV
    front_rows = SPAN * T_DEV
    query_3d = query_in.reshape(TOKENS, HEADS, HEAD_DIM)
    grad_3d = grad_out.reshape(TOKENS, HEADS, HEAD_DIM)
    pad_zero = jnp.zeros((front_rows, KV_HEADS * HEAD_DIM), key_in.dtype)
    key_pad = jnp.concatenate([pad_zero, key_in], axis=0).reshape(front_rows + TOKENS, KV_HEADS, HEAD_DIM)
    value_pad = jnp.concatenate([pad_zero, value_in], axis=0).reshape(front_rows + TOKENS, KV_HEADS, HEAD_DIM)

    def block_step(grad_carry, blk_idx):
        dk_grid, dv_grid = grad_carry
        row_start = (blk_idx * T_DEV).astype(jnp.int32)
        query_blk = lax.dynamic_slice_in_dim(query_3d, row_start, T_DEV, 0)
        grad_blk = lax.dynamic_slice_in_dim(grad_3d, row_start, T_DEV, 0)
        key_win = lax.dynamic_slice_in_dim(key_pad, row_start, win_blocks * T_DEV, 0)
        value_win = lax.dynamic_slice_in_dim(value_pad, row_start, win_blocks * T_DEV, 0)
        query_pos = row_start + jnp.arange(T_DEV, dtype=jnp.int32)
        key_pos = row_start - front_rows + jnp.arange(win_blocks * T_DEV, dtype=jnp.int32)
        visible = window_mask(query_pos, key_pos, doc_lengths)
        key_rep = jnp.repeat(key_win, group_size, axis=1)
        value_rep = jnp.repeat(value_win, group_size, axis=1)

        def one_head(items):
            return head_pass(items[0], items[1], items[2], items[3], visible, score_scale)
        attn_rows, grad_rows_q, part_dk, part_dv = lax.map(one_head, (query_blk.transpose(1, 0, 2), key_rep.transpose(1, 0, 2), value_rep.transpose(1, 0, 2), grad_blk.transpose(1, 0, 2)))
        part_dk = part_dk.reshape(KV_HEADS, group_size, win_blocks * T_DEV, HEAD_DIM).sum(axis=1).transpose(1, 0, 2)
        part_dv = part_dv.reshape(KV_HEADS, group_size, win_blocks * T_DEV, HEAD_DIM).sum(axis=1).transpose(1, 0, 2)
        dk_grid = lax.dynamic_update_slice_in_dim(dk_grid, lax.dynamic_slice_in_dim(dk_grid, row_start, win_blocks * T_DEV, 0) + part_dk, row_start, 0)
        dv_grid = lax.dynamic_update_slice_in_dim(dv_grid, lax.dynamic_slice_in_dim(dv_grid, row_start, win_blocks * T_DEV, 0) + part_dv, row_start, 0)
        return ((dk_grid, dv_grid), (attn_rows.transpose(1, 0, 2), grad_rows_q.transpose(1, 0, 2)))
    zero_grid = jnp.zeros((front_rows + TOKENS, KV_HEADS, HEAD_DIM), jnp.float32)
    (dk_grid, dv_grid), (out_blocks, dq_blocks) = lax.scan(block_step, (zero_grid, zero_grid), jnp.arange(num_blocks, dtype=jnp.int32))
    attn_out = out_blocks.reshape(TOKENS, HEADS * HEAD_DIM)
    grad_query = dq_blocks.reshape(TOKENS, HEADS * HEAD_DIM)
    grad_key = dk_grid[front_rows:].reshape(TOKENS, KV_HEADS * HEAD_DIM).astype(jnp.bfloat16)
    grad_value = dv_grid[front_rows:].reshape(TOKENS, KV_HEADS * HEAD_DIM).astype(jnp.bfloat16)
    return (attn_out, grad_query, grad_key, grad_value)
```

```python
import functools
import math

import jax
import jax.numpy as jnp
from jax import lax
from jax.experimental import pallas as pl
from jax.experimental.pallas import tpu as pltpu
from jax.sharding import PartitionSpec as P

MESH = pl.DeviceIdType.MESH
D = 128
SPAN = 3
WIN = SPAN + 1
ONES = 16
HIDDEN = -1e30
SCALE = 1.0 / math.sqrt(D)
SCALE_2 = SCALE * math.log2(math.e)
PAIR = 2


def dot(a, b):
    return jnp.dot(a, b, preferred_element_type=jnp.float32)


def dot_nt(a, b):
    return lax.dot_general(a, b, (((1,), (1,)), ((), ())), preferred_element_type=jnp.float32)


def kernel(
    n_seq,
    n_kvh,
    doc_ref,
    q_hbm,
    k_hbm,
    v_hbm,
    do_hbm,
    attn_ref,
    dq_ref,
    dk_ref,
    dv_ref,
    q_loc,
    do_loc,
    q_s,
    do_s,
    do_t,
    kv,
    k_t,
    v_t,
    bias,
    prob_s,
    max_s,
    out_t,
    attn_t,
    dq_t,
    ratio_s,
    delta_s,
    part,
    snd,
    rcv,
    local_sem,
    a2a_send,
    a2a_recv,
    halo_send,
    halo_recv,
    back_send,
    back_recv,
):
    rows, cols = do_loc.shape
    chunks, wide = q_s.shape[0], q_s.shape[1]
    pair = wide // rows
    per_half = chunks // 2
    piece = q_hbm.shape[0]
    s, g = lax.axis_index("seq"), lax.axis_index("kvh")
    nxt, prv = lax.rem(s + 1, n_seq), lax.rem(s + n_seq - 1, n_seq)

    def columns(h, width=D):
        return pl.ds(pl.multiple_of(h * width, width), width)

    mine = pl.ds(pl.multiple_of(g * piece, piece), piece)

    locals_ = [
        pltpu.make_async_copy(k_hbm.at[:, columns(g)], kv.at[SPAN, 0, mine, :], local_sem.at[0]),
        pltpu.make_async_copy(v_hbm.at[:, columns(g)], kv.at[SPAN, 1, mine, :], local_sem.at[1]),
        pltpu.make_async_copy(do_hbm, do_loc, local_sem.at[2]),
        pltpu.make_async_copy(q_hbm.at[:, columns(g, cols)], q_loc.at[mine, :], local_sem.at[3]),
    ]
    for copy in locals_:
        copy.start()

    barrier = pltpu.get_barrier_semaphore()
    for j in range(1, n_kvh):
        pl.semaphore_signal(
            barrier, inc=1, device_id=(s, lax.rem(g + j, n_kvh)), device_id_type=MESH
        )
    for to in (nxt, prv):
        pl.semaphore_signal(barrier, inc=1, device_id=(to, g), device_id_type=MESH)
    pl.semaphore_wait(barrier, n_kvh + 1)

    def to_peer(kind, j):
        peer = lax.rem(g + j, n_kvh)
        if kind >= 2:
            half = cols // 2
            src = q_hbm.at[:, columns(2 * peer + kind - 2, half)]
            dst = q_loc.at[mine, pl.ds((kind - 2) * half, half)]
        else:
            src = (k_hbm, v_hbm)[kind].at[:, columns(peer)]
            dst = kv.at[SPAN, kind, mine, :]
        return pltpu.make_async_remote_copy(
            src_ref=src,
            dst_ref=dst,
            send_sem=a2a_send.at[kind, j - 1],
            recv_sem=a2a_recv.at[kind, j - 1],
            device_id=(s, peer),
            device_id_type=MESH,
        )

    sends = [[to_peer(kind, j) for j in range(1, n_kvh)] for kind in range(4)]
    for kind in range(4):
        for copy in sends[kind]:
            copy.start()

    def halo(hop, kind):
        return pltpu.make_async_remote_copy(
            src_ref=kv.at[SPAN - hop, kind],
            dst_ref=kv.at[SPAN - hop - 1, kind],
            send_sem=halo_send.at[hop, kind],
            recv_sem=halo_recv.at[hop, kind],
            device_id=(nxt, g),
            device_id_type=MESH,
        )

    halos = [[halo(hop, kind) for kind in range(2)] for hop in range(SPAN)]

    def back(hop, kind):
        return pltpu.make_async_remote_copy(
            src_ref=snd.at[hop, kind],
            dst_ref=rcv.at[hop, kind],
            send_sem=back_send.at[hop, kind],
            recv_sem=back_recv.at[hop, kind],
            device_id=(prv, g),
            device_id_type=MESH,
        )

    backs = [[back(hop, kind) for kind in range(2)] for hop in range(SPAN)]

    docs = doc_ref.shape[1]
    lens = jnp.broadcast_to(doc_ref[...].astype(jnp.float32), (docs, docs))
    upto = lax.broadcasted_iota(jnp.int32, (docs, docs), 1) <= lax.broadcasted_iota(
        jnp.int32, (docs, docs), 0
    )
    ends = jnp.sum(jnp.where(upto, lens, 0.0), axis=1, keepdims=True)
    q_pos = (s * rows + lax.broadcasted_iota(jnp.int32, (1, rows), 1)).astype(jnp.float32)
    begin = jnp.max(jnp.where(ends <= q_pos, ends, 0.0), axis=0, keepdims=True)

    def set_up(w, _):
        k_pos = (
            (s - SPAN + w) * rows + lax.broadcasted_iota(jnp.int32, (rows, rows), 0)
        ).astype(jnp.float32)
        seen = (k_pos >= begin) & (k_pos <= q_pos)
        bias[w] = jnp.where(seen, 0.0, HIDDEN)
        v_t[w, D:, :] = jnp.ones((ONES, rows), jnp.bfloat16)
        part[w] = jnp.zeros(part.shape[1:], jnp.float32)
        return 0

    lax.fori_loop(0, WIN, set_up, 0)

    def clear(c, _):
        max_s[WIN, c] = jnp.full(max_s.shape[2:], HIDDEN, jnp.float32)
        out_t[c] = jnp.zeros(out_t.shape[1:], jnp.float32)
        dq_t[c] = jnp.zeros(dq_t.shape[1:], jnp.float32)
        return 0

    lax.fori_loop(0, chunks, clear, 0)

    def stack(src, dst, c):
        for u in range(pair):
            dst[c, u * rows : (u + 1) * rows, :] = src[:, columns(c * pair + u)]

    locals_[2].wait()

    def set_grad(c, _):
        stack(do_loc, do_s, c)
        do_t[c] = do_s[c].T
        return 0

    lax.fori_loop(0, chunks, set_grad, 0)

    def turn_kv(w):
        k_t[w] = kv[w, 0].T
        v_t[w, :D, :] = kv[w, 1].T

    def pass_on(hop, kind):
        halos[hop - 1][kind].wait_recv()
        halos[hop][kind].start()

    def take_queries(half):
        for copy in sends[2 + half]:
            copy.wait_recv()
        for c in range(per_half):
            stack(q_loc, q_s, half * per_half + c)

    for kind in range(2):
        locals_[kind].wait()
        for copy in sends[kind]:
            copy.wait_recv()
        halos[0][kind].start()
    turn_kv(SPAN)
    for kind in range(2):
        pass_on(1, kind)
    turn_kv(2)
    locals_[3].wait()
    take_queries(0)

    def forward(step, _):
        w, half = SPAN - step // 2, lax.rem(step, 2)

        @pl.when(step == 1)
        def _():
            take_queries(1)
            pass_on(2, 0)

        @pl.when(step == 2)
        def _():
            pass_on(2, 1)
            turn_kv(1)

        @pl.when(step == 2 * SPAN)
        def _():
            for kind in range(2):
                halos[2][kind].wait_recv()
            turn_kv(0)

        mask = jnp.concatenate([bias[w]] * pair, axis=1)
        mine_ = [half * per_half + c for c in range(per_half)]
        scores = [dot_nt(kv[w, 0], q_s[c]) + mask for c in mine_]
        for c, score in zip(mine_, scores):
            old = max_s[w + 1, c]
            top = jnp.maximum(jnp.max(score, axis=0, keepdims=True), old)
            max_s[w, c] = top
            prob = jnp.exp2(score * SCALE_2 - top * SCALE_2)
            prob_s[w, c] = prob
            add = dot(v_t[w], prob.astype(jnp.bfloat16))
            out_t[c] = out_t[c] * jnp.exp2((old - top) * SCALE_2) + add
        return 0

    lax.fori_loop(0, 2 * WIN, forward, 0)

    def finish(c, _):
        inv = 1.0 / out_t[c, D : D + 1, :]
        top = max_s[0, c]
        for w in range(WIN):
            ratio_s[w, c] = jnp.exp2((max_s[w, c] - top) * SCALE_2) * inv
        out = (out_t[c, :D, :] * inv).astype(jnp.bfloat16)
        attn_t[c] = out
        delta_s[c] = jnp.sum(
            out.astype(jnp.float32) * do_t[c].astype(jnp.float32), axis=0, keepdims=True
        )
        return 0

    lax.fori_loop(0, chunks, finish, 0)

    def pass_back(hop):
        for kind in (1, 0):
            total = part[hop, kind] * SCALE if kind == 0 else part[hop, kind]
            if hop > 0:
                backs[hop - 1][kind].wait_recv()
                total = total + rcv[hop - 1, kind].astype(jnp.float32)
            if hop < SPAN:
                snd[hop, kind] = total.astype(jnp.bfloat16)
                backs[hop][kind].start()
            else:
                (dk_ref, dv_ref)[kind][...] = total.astype(jnp.bfloat16)

    def unturn(src, dst, scale):
        def one(c, _):
            for u in range(pair):
                part_ = src[c, :, u * rows : (u + 1) * rows]
                if scale is not None:
                    part_ = (part_ * scale).astype(jnp.bfloat16)
                dst[:, columns(c * pair + u)] = part_.T
            return 0

        lax.fori_loop(0, chunks, one, 0)

    def backward(step, _):
        w, half = step // 2, lax.rem(step, 2)
        mine_ = [half * per_half + c for c in range(per_half)]
        grads = [dot(kv[w, 1], do_t[c]) for c in mine_]
        for c, grad in zip(mine_, grads):
            prob = prob_s[w, c] * ratio_s[w, c]
            ds = (prob * (grad - delta_s[c])).astype(jnp.bfloat16)
            part[w, 1] += dot(prob.astype(jnp.bfloat16), do_s[c])
            part[w, 0] += dot(ds, q_s[c])
            dq_t[c] += dot(k_t[w], ds)

        for hop in range(SPAN):

            @pl.when(step == 2 * hop + 1)
            def _(hop=hop):
                if hop == 1:
                    unturn(attn_t, attn_ref, None)
                pass_back(hop)

        return 0

    lax.fori_loop(0, 2 * WIN, backward, 0)
    unturn(dq_t, dq_ref, SCALE)
    pass_back(SPAN)

    for group in sends + halos + backs:
        for copy in group:
            copy.wait_send()


def settle(*refs):
    n = len(refs) // 2
    copies = [
        pltpu.make_async_copy(refs[i], refs[n + i], refs[-1].at[i]) for i in range(n)
    ]
    for copy in copies:
        copy.start()
    for copy in copies:
        copy.wait()


def per_device(n_seq, n_kvh, query_in, key_in, value_in, grad_out, doc_lengths):
    rows, cols = grad_out.shape
    chunks, wide = cols // (D * PAIR), PAIR * rows
    bf16, f32 = jnp.bfloat16, jnp.float32
    vmem = pl.BlockSpec(memory_space=pltpu.VMEM)
    hbm = pl.BlockSpec(memory_space=pltpu.HBM)
    dma = pltpu.SemaphoreType.DMA
    shapes = (
        jax.ShapeDtypeStruct((rows, cols), bf16),
        jax.ShapeDtypeStruct((rows, cols), bf16),
        jax.ShapeDtypeStruct((rows, D), bf16),
        jax.ShapeDtypeStruct((rows, D), bf16),
    )
    results = pl.pallas_call(
        functools.partial(kernel, n_seq, n_kvh),
        out_shape=tuple(pltpu.VMEM(shape.shape, shape.dtype) for shape in shapes),
        in_specs=[vmem, hbm, hbm, hbm, hbm],
        out_specs=(vmem, vmem, vmem, vmem),
        scratch_shapes=[
            pltpu.VMEM((rows, cols), bf16),
            pltpu.VMEM((rows, cols), bf16),
            pltpu.VMEM((chunks, wide, D), bf16),
            pltpu.VMEM((chunks, wide, D), bf16),
            pltpu.VMEM((chunks, D, wide), bf16),
            pltpu.VMEM((WIN, 2, rows, D), bf16),
            pltpu.VMEM((WIN, D, rows), bf16),
            pltpu.VMEM((WIN, D + ONES, rows), bf16),
            pltpu.VMEM((WIN, rows, rows), f32),
            pltpu.VMEM((WIN, chunks, rows, wide), f32),
            pltpu.VMEM((WIN + 1, chunks, 1, wide), f32),
            pltpu.VMEM((chunks, D + ONES, wide), f32),
            pltpu.VMEM((chunks, D, wide), bf16),
            pltpu.VMEM((chunks, D, wide), f32),
            pltpu.VMEM((WIN, chunks, 1, wide), f32),
            pltpu.VMEM((chunks, 1, wide), f32),
            pltpu.VMEM((WIN, 2, rows, D), f32),
            pltpu.VMEM((SPAN, 2, rows, D), bf16),
            pltpu.VMEM((SPAN, 2, rows, D), bf16),
            dma((4,)),
            dma((4, n_kvh - 1)),
            dma((4, n_kvh - 1)),
            dma((SPAN, 2)),
            dma((SPAN, 2)),
            dma((SPAN, 2)),
            dma((SPAN, 2)),
        ],
        compiler_params=pltpu.CompilerParams(
            collective_id=0, has_side_effects=True, vmem_limit_bytes=48 * 1024 * 1024
        ),
    )(
        *(
            pltpu.with_memory_space_constraint(operand, pltpu.HBM)
            for operand in (doc_lengths.reshape(1, -1), query_in, key_in, value_in, grad_out)
        )
    )
    return pl.pallas_call(
        settle,
        out_shape=shapes,
        in_specs=[vmem] * len(shapes),
        out_specs=(hbm,) * len(shapes),
        scratch_shapes=[dma((len(shapes),))],
    )(*(pltpu.with_memory_space_constraint(result, pltpu.VMEM) for result in results))


def solution(mesh):
    placed = (
        P(("seq", "kvh"), None),
        P(("seq", "kvh"), None),
        P(("seq", "kvh"), None),
        P("seq", "kvh"),
        P(),
    )
    return jax.shard_map(
        functools.partial(per_device, mesh.shape["seq"], mesh.shape["kvh"]),
        mesh=mesh,
        in_specs=placed,
        out_specs=(P("seq", "kvh"), P("seq", "kvh"), P("seq", "kvh"), P("seq", "kvh")),
        check_vma=False,
    )
```

```python
import functools
import math

import jax
import jax.numpy as jnp
from jax import lax
from jax.experimental import pallas as pl
from jax.experimental.pallas import tpu as pltpu
from jax.sharding import PartitionSpec as P

MESH = pl.DeviceIdType.MESH
D = 128
SPAN = 3
WIN = SPAN + 1
ONES = 16
HIDDEN = -1e30
SCALE = 1.0 / math.sqrt(D)
SCALE_2 = SCALE * math.log2(math.e)
PAIR = 2


def dot(a, b):
    return jnp.dot(a, b, preferred_element_type=jnp.float32)


def kernel(
    n_seq,
    n_kvh,
    doc_ref,
    q_hbm,
    k_hbm,
    v_hbm,
    do_hbm,
    attn_ref,
    dq_ref,
    dk_ref,
    dv_ref,
    q_loc,
    do_loc,
    q_s,
    q_t,
    do_s,
    do_t,
    kv,
    k_t,
    v_t,
    bias,
    prob_s,
    max_s,
    out_t,
    attn_t,
    dq_t,
    ratio_s,
    delta_s,
    part,
    snd,
    rcv,
    local_sem,
    a2a_send,
    a2a_recv,
    halo_send,
    halo_recv,
    back_send,
    back_recv,
):
    rows, cols = do_loc.shape
    chunks, wide = q_s.shape[0], q_s.shape[1]
    pair = wide // rows
    per_half = chunks // 2
    piece = q_hbm.shape[0]
    s, g = lax.axis_index("seq"), lax.axis_index("kvh")
    nxt, prv = lax.rem(s + 1, n_seq), lax.rem(s + n_seq - 1, n_seq)

    def columns(h, width=D):
        return pl.ds(pl.multiple_of(h * width, width), width)

    mine = pl.ds(pl.multiple_of(g * piece, piece), piece)

    locals_ = [
        pltpu.make_async_copy(k_hbm.at[:, columns(g)], kv.at[SPAN, 0, mine, :], local_sem.at[0]),
        pltpu.make_async_copy(v_hbm.at[:, columns(g)], kv.at[SPAN, 1, mine, :], local_sem.at[1]),
        pltpu.make_async_copy(do_hbm, do_loc, local_sem.at[2]),
        pltpu.make_async_copy(q_hbm.at[:, columns(g, cols)], q_loc.at[mine, :], local_sem.at[3]),
    ]
    for copy in locals_:
        copy.start()

    barrier = pltpu.get_barrier_semaphore()
    for j in range(1, n_kvh):
        pl.semaphore_signal(
            barrier, inc=1, device_id=(s, lax.rem(g + j, n_kvh)), device_id_type=MESH
        )
    for to in (nxt, prv):
        pl.semaphore_signal(barrier, inc=1, device_id=(to, g), device_id_type=MESH)
    pl.semaphore_wait(barrier, n_kvh + 1)

    def to_peer(kind, j):
        peer = lax.rem(g + j, n_kvh)
        if kind >= 2:
            half = cols // 2
            src = q_hbm.at[:, columns(2 * peer + kind - 2, half)]
            dst = q_loc.at[mine, pl.ds((kind - 2) * half, half)]
        else:
            src = (k_hbm, v_hbm)[kind].at[:, columns(peer)]
            dst = kv.at[SPAN, kind, mine, :]
        return pltpu.make_async_remote_copy(
            src_ref=src,
            dst_ref=dst,
            send_sem=a2a_send.at[kind, j - 1],
            recv_sem=a2a_recv.at[kind, j - 1],
            device_id=(s, peer),
            device_id_type=MESH,
        )

    sends = [[to_peer(kind, j) for j in range(1, n_kvh)] for kind in range(4)]

    def start(copies):
        for copy in copies:
            copy.start()

    def halo(hop, kind):
        return pltpu.make_async_remote_copy(
            src_ref=kv.at[SPAN - hop, kind],
            dst_ref=kv.at[SPAN - hop - 1, kind],
            send_sem=halo_send.at[hop, kind],
            recv_sem=halo_recv.at[hop, kind],
            device_id=(nxt, g),
            device_id_type=MESH,
        )

    halos = [[halo(hop, kind) for kind in range(2)] for hop in range(SPAN)]

    def back(hop, kind):
        return pltpu.make_async_remote_copy(
            src_ref=snd.at[hop, kind],
            dst_ref=rcv.at[hop, kind],
            send_sem=back_send.at[hop, kind],
            recv_sem=back_recv.at[hop, kind],
            device_id=(prv, g),
            device_id_type=MESH,
        )

    backs = [[back(hop, kind) for kind in range(2)] for hop in range(SPAN)]

    def stack(src, dst, c):
        for u in range(pair):
            dst[c, u * rows : (u + 1) * rows, :] = src[:, columns(c * pair + u)]

    def turn_kv(w):
        k_t[w] = kv[w, 0].T
        v_t[w, :D, :] = kv[w, 1].T

    def pass_on(hop, kind):
        halos[hop - 1][kind].wait_recv()
        halos[hop][kind].start()

    def take_queries(half):
        for copy in sends[2 + half]:
            copy.wait_recv()
        for c in range(half * per_half, (half + 1) * per_half):
            stack(q_loc, q_s, c)
            q_t[c] = q_s[c].T

    def set_all():
        docs = doc_ref.shape[1]
        lens = jnp.broadcast_to(doc_ref[...].astype(jnp.float32), (docs, docs))
        upto = lax.broadcasted_iota(jnp.int32, (docs, docs), 1) <= lax.broadcasted_iota(
            jnp.int32, (docs, docs), 0
        )
        ends = jnp.sum(jnp.where(upto, lens, 0.0), axis=1, keepdims=True)
        q_pos = (s * rows + lax.broadcasted_iota(jnp.int32, (1, rows), 1)).astype(jnp.float32)
        begin = jnp.max(jnp.where(ends <= q_pos, ends, 0.0), axis=0, keepdims=True)

        def set_up(w, _):
            k_pos = (
                (s - SPAN + w) * rows + lax.broadcasted_iota(jnp.int32, (rows, rows), 0)
            ).astype(jnp.float32)
            seen = (k_pos >= begin) & (k_pos <= q_pos)
            bias[w] = jnp.where(seen, 0.0, HIDDEN)
            v_t[w, D:, :] = jnp.ones((ONES, rows), jnp.bfloat16)
            part[w] = jnp.zeros(part.shape[1:], jnp.float32)
            return 0

        lax.fori_loop(0, WIN, set_up, 0)

        def clear(c, _):
            max_s[WIN, c] = jnp.full(max_s.shape[2:], HIDDEN, jnp.float32)
            out_t[c] = jnp.zeros(out_t.shape[1:], jnp.float32)
            dq_t[c] = jnp.zeros(dq_t.shape[1:], jnp.float32)
            return 0

        lax.fori_loop(0, chunks, clear, 0)

        locals_[2].wait()

        def set_grad(c, _):
            stack(do_loc, do_s, c)
            do_t[c] = do_s[c].T
            return 0

        lax.fori_loop(0, chunks, set_grad, 0)

    def piece_on(kind, j):
        place = (
            pl.ds(pl.multiple_of(lax.rem(g + n_kvh - j, n_kvh) * piece, piece), piece),
            slice(None),
        )
        pltpu.make_async_remote_copy(
            src_ref=kv.at[(SPAN, kind) + place],
            dst_ref=kv.at[(SPAN - 1, kind) + place],
            send_sem=halo_send.at[0, kind],
            recv_sem=halo_recv.at[0, kind],
            device_id=(nxt, g),
            device_id_type=MESH,
        ).start()

    near_first = sorted(range(1, n_kvh), key=lambda j: min(j, n_kvh - j))
    for kind in range(2):
        start(sends[kind])
    for kind in range(2):
        locals_[kind].wait()
        piece_on(kind, 0)
    for kind in range(2):
        for j in near_first:
            sends[kind][j - 1].wait_recv()
            piece_on(kind, j)
        start(sends[2 + kind])

    set_all()
    turn_kv(SPAN)
    pass_on(1, 0)
    pass_on(1, 1)
    turn_kv(SPAN - 1)
    pass_on(2, 0)
    locals_[3].wait()
    take_queries(0)

    def weigh(w, c, score):
        old = max_s[w + 1, c]
        top = jnp.maximum(jnp.max(score, axis=0, keepdims=True), old)
        max_s[w, c] = top
        prob = jnp.exp2(score * SCALE_2 - top * SCALE_2)
        prob_s[w, c] = prob
        return prob

    def gather(w, c, prob):
        shrink = jnp.exp2((max_s[w + 1, c] - max_s[w, c]) * SCALE_2)
        out_t[c] = out_t[c] * shrink + dot(v_t[w], prob.astype(jnp.bfloat16))

    def chunks_of(half):
        return [half * per_half + c for c in range(per_half)]

    def scores(w, half):
        mask = jnp.concatenate([bias[w]] * pair, axis=1)
        return [dot(kv[w, 0], q_t[c]) + mask for c in chunks_of(half)]

    def forward(step, _):
        early = 1 - step // 4
        w = SPAN - early * lax.rem(step, 2) - (1 - early) * 2
        half = early * (step // 2) + (1 - early) * lax.rem(step, 2)

        @pl.when(step == 1)
        def _():
            pass_on(2, 1)

        @pl.when(step == 2)
        def _():
            take_queries(1)

        @pl.when(step == 4)
        def _():
            turn_kv(1)

        for c, score in zip(chunks_of(half), scores(w, half)):
            gather(w, c, weigh(w, c, score))
        return 0

    lax.fori_loop(0, 6, forward, 0)

    def oldest_scores(half, _):
        for c, score in zip(chunks_of(half), scores(0, half)):
            weigh(0, c, score)
        return 0

    halos[2][0].wait_recv()
    lax.fori_loop(0, 2, oldest_scores, 0)
    halos[2][1].wait_recv()
    turn_kv(0)

    def oldest_sum(c, _):
        gather(0, c, prob_s[0, c])
        return 0

    lax.fori_loop(0, chunks, oldest_sum, 0)

    def finish(c, _):
        inv = 1.0 / out_t[c, D : D + 1, :]
        top = max_s[0, c]
        for w in range(WIN):
            ratio_s[w, c] = jnp.exp2((max_s[w, c] - top) * SCALE_2) * inv
        out = (out_t[c, :D, :] * inv).astype(jnp.bfloat16)
        attn_t[c] = out
        delta_s[c] = jnp.sum(
            out.astype(jnp.float32) * do_t[c].astype(jnp.float32), axis=0, keepdims=True
        )
        return 0

    lax.fori_loop(0, chunks, finish, 0)

    def pass_back(hop, kinds=(1, 0)):
        for kind in kinds:
            total = part[hop, kind] * SCALE if kind == 0 else part[hop, kind]
            if hop > 0:
                backs[hop - 1][kind].wait_recv()
                total = total + rcv[hop - 1, kind].astype(jnp.float32)
            if hop < SPAN:
                snd[hop, kind] = total.astype(jnp.bfloat16)
                backs[hop][kind].start()
            else:
                (dk_ref, dv_ref)[kind][...] = total.astype(jnp.bfloat16)

    def unturn(src, dst, scale):
        def one(c, _):
            for u in range(pair):
                part_ = src[c, :, u * rows : (u + 1) * rows]
                if scale is not None:
                    part_ = (part_ * scale).astype(jnp.bfloat16)
                dst[:, columns(c * pair + u)] = part_.T
            return 0

        lax.fori_loop(0, chunks, one, 0)

    def one_dv(w, c, prob):
        part[w, 1] += dot(prob.astype(jnp.bfloat16), do_s[c])

    def one_dk(w, c, prob, grad):
        ds = (prob * (grad - delta_s[c])).astype(jnp.bfloat16)
        part[w, 0] += dot(ds, q_s[c])
        dq_t[c] += dot(k_t[w], ds)

    def oldest_dv(half, _):
        for c in chunks_of(half):
            one_dv(0, c, prob_s[0, c] * ratio_s[0, c])
        return 0

    def oldest_dk(half, _):
        grads = [dot(kv[0, 1], do_t[c]) for c in chunks_of(half)]
        for c, grad in zip(chunks_of(half), grads):
            one_dk(0, c, prob_s[0, c] * ratio_s[0, c], grad)
        return 0

    lax.fori_loop(0, 2, oldest_dv, 0)
    pass_back(0, (1,))
    lax.fori_loop(0, 2, oldest_dk, 0)
    pass_back(0, (0,))

    def backward(step, _):
        w, half = step // 2, lax.rem(step, 2)
        grads = [dot(kv[w, 1], do_t[c]) for c in chunks_of(half)]
        for c, grad in zip(chunks_of(half), grads):
            prob = prob_s[w, c] * ratio_s[w, c]
            one_dv(w, c, prob)
            one_dk(w, c, prob, grad)

        for hop in range(1, SPAN):

            @pl.when(step == 2 * hop + 1)
            def _(hop=hop):
                if hop == 1:
                    unturn(attn_t, attn_ref, None)
                pass_back(hop)

        return 0

    lax.fori_loop(2, 2 * WIN, backward, 0)
    unturn(dq_t, dq_ref, SCALE)
    pass_back(SPAN)

    for group in sends + halos + backs:
        for copy in group:
            copy.wait_send()


def settle(*refs):
    n = len(refs) // 2
    copies = [
        pltpu.make_async_copy(refs[i], refs[n + i], refs[-1].at[i]) for i in range(n)
    ]
    for copy in copies:
        copy.start()
    for copy in copies:
        copy.wait()


def per_device(n_seq, n_kvh, query_in, key_in, value_in, grad_out, doc_lengths):
    rows, cols = grad_out.shape
    chunks, wide = cols // (D * PAIR), PAIR * rows
    bf16, f32 = jnp.bfloat16, jnp.float32
    vmem = pl.BlockSpec(memory_space=pltpu.VMEM)
    hbm = pl.BlockSpec(memory_space=pltpu.HBM)
    dma = pltpu.SemaphoreType.DMA
    shapes = (
        jax.ShapeDtypeStruct((rows, cols), bf16),
        jax.ShapeDtypeStruct((rows, cols), bf16),
        jax.ShapeDtypeStruct((rows, D), bf16),
        jax.ShapeDtypeStruct((rows, D), bf16),
    )
    results = pl.pallas_call(
        functools.partial(kernel, n_seq, n_kvh),
        out_shape=tuple(pltpu.VMEM(shape.shape, shape.dtype) for shape in shapes),
        in_specs=[vmem, hbm, hbm, hbm, hbm],
        out_specs=(vmem, vmem, vmem, vmem),
        scratch_shapes=[
            pltpu.VMEM((rows, cols), bf16),
            pltpu.VMEM((rows, cols), bf16),
            pltpu.VMEM((chunks, wide, D), bf16),
            pltpu.VMEM((chunks, D, wide), bf16),
            pltpu.VMEM((chunks, wide, D), bf16),
            pltpu.VMEM((chunks, D, wide), bf16),
            pltpu.VMEM((WIN, 2, rows, D), bf16),
            pltpu.VMEM((WIN, D, rows), bf16),
            pltpu.VMEM((WIN, D + ONES, rows), bf16),
            pltpu.VMEM((WIN, rows, rows), f32),
            pltpu.VMEM((WIN, chunks, rows, wide), f32),
            pltpu.VMEM((WIN + 1, chunks, 1, wide), f32),
            pltpu.VMEM((chunks, D + ONES, wide), f32),
            pltpu.VMEM((chunks, D, wide), bf16),
            pltpu.VMEM((chunks, D, wide), f32),
            pltpu.VMEM((WIN, chunks, 1, wide), f32),
            pltpu.VMEM((chunks, 1, wide), f32),
            pltpu.VMEM((WIN, 2, rows, D), f32),
            pltpu.VMEM((SPAN, 2, rows, D), bf16),
            pltpu.VMEM((SPAN, 2, rows, D), bf16),
            dma((4,)),
            dma((4, n_kvh - 1)),
            dma((4, n_kvh - 1)),
            dma((SPAN, 2)),
            dma((SPAN, 2)),
            dma((SPAN, 2)),
            dma((SPAN, 2)),
        ],
        compiler_params=pltpu.CompilerParams(
            collective_id=0, has_side_effects=True, vmem_limit_bytes=48 * 1024 * 1024
        ),
    )(
        *(
            pltpu.with_memory_space_constraint(operand, pltpu.HBM)
            for operand in (doc_lengths.reshape(1, -1), query_in, key_in, value_in, grad_out)
        )
    )
    return pl.pallas_call(
        settle,
        out_shape=shapes,
        in_specs=[vmem] * len(shapes),
        out_specs=(hbm,) * len(shapes),
        scratch_shapes=[dma((len(shapes),))],
    )(*(pltpu.with_memory_space_constraint(result, pltpu.VMEM) for result in results))


def solution(mesh):
    placed = (
        P(("seq", "kvh"), None),
        P(("seq", "kvh"), None),
        P(("seq", "kvh"), None),
        P("seq", "kvh"),
        P(),
    )
    return jax.shard_map(
        functools.partial(per_device, mesh.shape["seq"], mesh.shape["kvh"]),
        mesh=mesh,
        in_specs=placed,
        out_specs=(P("seq", "kvh"), P("seq", "kvh"), P("seq", "kvh"), P("seq", "kvh")),
        check_vma=False,
    )
```

```python
import functools
import math

import jax
import jax.numpy as jnp
from jax import lax
from jax.experimental import pallas as pl
from jax.experimental.pallas import tpu as pltpu
from jax.sharding import PartitionSpec as P

MESH = pl.DeviceIdType.MESH
D = 128
SPAN = 3
WIN = SPAN + 1
ONES = 16
HIDDEN = -1e30
SCALE = 1.0 / math.sqrt(D)
SCALE_2 = SCALE * math.log2(math.e)
PAIR = 2


def dot(a, b):
    return jnp.dot(a, b, preferred_element_type=jnp.float32)


def dot_nt(a, b):
    return lax.dot_general(a, b, (((1,), (1,)), ((), ())), preferred_element_type=jnp.float32)


def kernel(
    n_seq,
    n_kvh,
    doc_ref,
    q_hbm,
    k_hbm,
    v_hbm,
    do_hbm,
    attn_ref,
    dq_ref,
    dk_ref,
    dv_ref,
    q_loc,
    do_loc,
    q_t,
    do_t,
    kv,
    k_t,
    v_t,
    bias,
    prob_s,
    max_s,
    out_t,
    attn_t,
    dq_t,
    ratio_s,
    delta_s,
    part,
    snd,
    rcv,
    local_sem,
    a2a_send,
    a2a_recv,
    halo_send,
    halo_recv,
    back_send,
    back_recv,
):
    rows, cols = do_loc.shape
    chunks, wide = q_t.shape[0], q_t.shape[2]
    pair = wide // rows
    per_half = chunks // 2
    piece = q_hbm.shape[0]
    s, g = lax.axis_index("seq"), lax.axis_index("kvh")
    nxt, prv = lax.rem(s + 1, n_seq), lax.rem(s + n_seq - 1, n_seq)

    def columns(h, width=D):
        return pl.ds(pl.multiple_of(h * width, width), width)

    mine = pl.ds(pl.multiple_of(g * piece, piece), piece)

    locals_ = [
        pltpu.make_async_copy(k_hbm.at[:, columns(g)], kv.at[SPAN, 0, mine, :], local_sem.at[0]),
        pltpu.make_async_copy(v_hbm.at[:, columns(g)], kv.at[SPAN, 1, mine, :], local_sem.at[1]),
        pltpu.make_async_copy(do_hbm, do_loc, local_sem.at[2]),
        pltpu.make_async_copy(q_hbm.at[:, columns(g, cols)], q_loc.at[mine, :], local_sem.at[3]),
    ]
    for copy in locals_:
        copy.start()

    barrier = pltpu.get_barrier_semaphore()
    for j in range(1, n_kvh):
        pl.semaphore_signal(
            barrier, inc=1, device_id=(s, lax.rem(g + j, n_kvh)), device_id_type=MESH
        )
    for to in (nxt, prv):
        pl.semaphore_signal(barrier, inc=1, device_id=(to, g), device_id_type=MESH)
    pl.semaphore_wait(barrier, n_kvh + 1)

    def to_peer(kind, j):
        peer = lax.rem(g + j, n_kvh)
        if kind >= 2:
            half = cols // 2
            src = q_hbm.at[:, columns(2 * peer + kind - 2, half)]
            dst = q_loc.at[mine, pl.ds((kind - 2) * half, half)]
        else:
            src = (k_hbm, v_hbm)[kind].at[:, columns(peer)]
            dst = kv.at[SPAN, kind, mine, :]
        return pltpu.make_async_remote_copy(
            src_ref=src,
            dst_ref=dst,
            send_sem=a2a_send.at[kind, j - 1],
            recv_sem=a2a_recv.at[kind, j - 1],
            device_id=(s, peer),
            device_id_type=MESH,
        )

    sends = [[to_peer(kind, j) for j in range(1, n_kvh)] for kind in range(4)]

    def start(copies):
        for copy in copies:
            copy.start()

    def halo(hop, kind):
        return pltpu.make_async_remote_copy(
            src_ref=kv.at[SPAN - hop, kind],
            dst_ref=kv.at[SPAN - hop - 1, kind],
            send_sem=halo_send.at[hop, kind],
            recv_sem=halo_recv.at[hop, kind],
            device_id=(nxt, g),
            device_id_type=MESH,
        )

    halos = [[halo(hop, kind) for kind in range(2)] for hop in range(SPAN)]

    def back(hop, kind):
        return pltpu.make_async_remote_copy(
            src_ref=snd.at[hop, kind],
            dst_ref=rcv.at[hop, kind],
            send_sem=back_send.at[hop, kind],
            recv_sem=back_recv.at[hop, kind],
            device_id=(prv, g),
            device_id_type=MESH,
        )

    backs = [[back(hop, kind) for kind in range(2)] for hop in range(SPAN)]

    def turn(src, dst, c):
        for u in range(pair):
            dst[c, :, u * rows : (u + 1) * rows] = src[:, columns(c * pair + u)].T

    def turn_kv(w):
        k_t[w] = kv[w, 0].T
        v_t[w, :D, :] = kv[w, 1].T

    def pass_on(hop, kind):
        halos[hop - 1][kind].wait_recv()
        halos[hop][kind].start()

    def take_queries(half):
        for copy in sends[2 + half]:
            copy.wait_recv()
        for c in range(half * per_half, (half + 1) * per_half):
            turn(q_loc, q_t, c)

    def set_all():
        docs = doc_ref.shape[1]
        lens = jnp.broadcast_to(doc_ref[...].astype(jnp.float32), (docs, docs))
        upto = lax.broadcasted_iota(jnp.int32, (docs, docs), 1) <= lax.broadcasted_iota(
            jnp.int32, (docs, docs), 0
        )
        ends = jnp.sum(jnp.where(upto, lens, 0.0), axis=1, keepdims=True)
        q_pos = (s * rows + lax.broadcasted_iota(jnp.int32, (1, rows), 1)).astype(jnp.float32)
        begin = jnp.max(jnp.where(ends <= q_pos, ends, 0.0), axis=0, keepdims=True)

        def set_up(w, _):
            k_pos = (
                (s - SPAN + w) * rows + lax.broadcasted_iota(jnp.int32, (rows, rows), 0)
            ).astype(jnp.float32)
            seen = (k_pos >= begin) & (k_pos <= q_pos)
            bias[w] = jnp.where(seen, 0.0, HIDDEN)
            v_t[w, D:, :] = jnp.ones((ONES, rows), jnp.bfloat16)
            part[w] = jnp.zeros(part.shape[1:], jnp.float32)
            return 0

        lax.fori_loop(0, WIN, set_up, 0)

        def clear(c, _):
            max_s[WIN, c] = jnp.full(max_s.shape[2:], HIDDEN, jnp.float32)
            out_t[c] = jnp.zeros(out_t.shape[1:], jnp.float32)
            dq_t[c] = jnp.zeros(dq_t.shape[1:], jnp.float32)
            return 0

        lax.fori_loop(0, chunks, clear, 0)

        locals_[2].wait()

        def set_grad(c, _):
            turn(do_loc, do_t, c)
            return 0

        lax.fori_loop(0, chunks, set_grad, 0)

    def piece_on(kind, j):
        place = (
            pl.ds(pl.multiple_of(lax.rem(g + n_kvh - j, n_kvh) * piece, piece), piece),
            slice(None),
        )
        pltpu.make_async_remote_copy(
            src_ref=kv.at[(SPAN, kind) + place],
            dst_ref=kv.at[(SPAN - 1, kind) + place],
            send_sem=halo_send.at[0, kind],
            recv_sem=halo_recv.at[0, kind],
            device_id=(nxt, g),
            device_id_type=MESH,
        ).start()

    near_first = sorted(range(1, n_kvh), key=lambda j: min(j, n_kvh - j))
    for kind in range(2):
        start(sends[kind])
    for kind in range(2):
        locals_[kind].wait()
        piece_on(kind, 0)
    for kind in range(2, 4):
        start(sends[kind])
    for kind in range(2):
        for j in near_first:
            sends[kind][j - 1].wait_recv()
            piece_on(kind, j)

    set_all()
    turn_kv(SPAN)
    pass_on(1, 0)
    pass_on(1, 1)
    turn_kv(SPAN - 1)
    pass_on(2, 0)
    locals_[3].wait()
    take_queries(0)

    def weigh(w, c, score):
        old = max_s[w + 1, c]
        top = jnp.maximum(jnp.max(score, axis=0, keepdims=True), old)
        max_s[w, c] = top
        prob = jnp.exp2(score * SCALE_2 - top * SCALE_2)
        prob_s[w, c] = prob
        return prob

    def gather(w, c, prob):
        shrink = jnp.exp2((max_s[w + 1, c] - max_s[w, c]) * SCALE_2)
        out_t[c] = out_t[c] * shrink + dot(v_t[w], prob.astype(jnp.bfloat16))

    def chunks_of(half):
        return [half * per_half + c for c in range(per_half)]

    def scores(w, half):
        mask = jnp.concatenate([bias[w]] * pair, axis=1)
        return [dot(kv[w, 0], q_t[c]) + mask for c in chunks_of(half)]

    def forward(step, _):
        early = 1 - step // 4
        w = SPAN - early * lax.rem(step, 2) - (1 - early) * 2
        half = early * (step // 2) + (1 - early) * lax.rem(step, 2)

        @pl.when(step == 1)
        def _():
            pass_on(2, 1)

        @pl.when(step == 2)
        def _():
            take_queries(1)

        @pl.when(step == 4)
        def _():
            turn_kv(1)

        for c, score in zip(chunks_of(half), scores(w, half)):
            gather(w, c, weigh(w, c, score))
        return 0

    lax.fori_loop(0, 6, forward, 0)

    def oldest_scores(half, _):
        for c, score in zip(chunks_of(half), scores(0, half)):
            weigh(0, c, score)
        return 0

    halos[2][0].wait_recv()
    lax.fori_loop(0, 2, oldest_scores, 0)
    halos[2][1].wait_recv()
    turn_kv(0)

    def oldest_sum(c, _):
        gather(0, c, prob_s[0, c])
        return 0

    lax.fori_loop(0, chunks, oldest_sum, 0)

    def finish(c, _):
        inv = 1.0 / out_t[c, D : D + 1, :]
        top = max_s[0, c]
        for w in range(WIN):
            ratio_s[w, c] = jnp.exp2((max_s[w, c] - top) * SCALE_2) * inv
        out = (out_t[c, :D, :] * inv).astype(jnp.bfloat16)
        attn_t[c] = out
        delta_s[c] = jnp.sum(
            out.astype(jnp.float32) * do_t[c].astype(jnp.float32), axis=0, keepdims=True
        )
        return 0

    lax.fori_loop(0, chunks, finish, 0)

    def pass_back(hop, kinds=(1, 0)):
        for kind in kinds:
            total = part[hop, kind] * SCALE if kind == 0 else part[hop, kind]
            if hop > 0:
                backs[hop - 1][kind].wait_recv()
                total = total + rcv[hop - 1, kind].astype(jnp.float32)
            if hop < SPAN:
                snd[hop, kind] = total.astype(jnp.bfloat16)
                backs[hop][kind].start()
            else:
                (dk_ref, dv_ref)[kind][...] = total.astype(jnp.bfloat16).T

    def unturn(src, dst, scale):
        def one(c, _):
            for u in range(pair):
                part_ = src[c, :, u * rows : (u + 1) * rows]
                if scale is not None:
                    part_ = (part_ * scale).astype(jnp.bfloat16)
                dst[:, columns(c * pair + u)] = part_.T
            return 0

        lax.fori_loop(0, chunks, one, 0)

    def one_dv(w, c, prob):
        part[w, 1] += dot_nt(do_t[c], prob.astype(jnp.bfloat16))

    def one_dk(w, c, prob, grad):
        ds = (prob * (grad - delta_s[c])).astype(jnp.bfloat16)
        part[w, 0] += dot_nt(q_t[c], ds)
        dq_t[c] += dot(k_t[w], ds)

    def oldest_dv(half, _):
        for c in chunks_of(half):
            one_dv(0, c, prob_s[0, c] * ratio_s[0, c])
        return 0

    def oldest_dk(half, _):
        grads = [dot(kv[0, 1], do_t[c]) for c in chunks_of(half)]
        for c, grad in zip(chunks_of(half), grads):
            one_dk(0, c, prob_s[0, c] * ratio_s[0, c], grad)
        return 0

    lax.fori_loop(0, 2, oldest_dv, 0)
    pass_back(0, (1,))
    lax.fori_loop(0, 2, oldest_dk, 0)
    pass_back(0, (0,))

    def backward(step, _):
        w, half = step // 2, lax.rem(step, 2)
        grads = [dot(kv[w, 1], do_t[c]) for c in chunks_of(half)]
        for c, grad in zip(chunks_of(half), grads):
            prob = prob_s[w, c] * ratio_s[w, c]
            one_dv(w, c, prob)
            one_dk(w, c, prob, grad)

        for hop in range(1, SPAN):

            @pl.when(step == 2 * hop + 1)
            def _(hop=hop):
                if hop == 1:
                    unturn(attn_t, attn_ref, None)
                pass_back(hop)

        return 0

    lax.fori_loop(2, 2 * WIN, backward, 0)
    unturn(dq_t, dq_ref, SCALE)
    pass_back(SPAN)

    for group in sends + halos + backs:
        for copy in group:
            copy.wait_send()


def settle(*refs):
    n = len(refs) // 2
    copies = [
        pltpu.make_async_copy(refs[i], refs[n + i], refs[-1].at[i]) for i in range(n)
    ]
    for copy in copies:
        copy.start()
    for copy in copies:
        copy.wait()


def per_device(n_seq, n_kvh, query_in, key_in, value_in, grad_out, doc_lengths):
    rows, cols = grad_out.shape
    chunks, wide = cols // (D * PAIR), PAIR * rows
    bf16, f32 = jnp.bfloat16, jnp.float32
    vmem = pl.BlockSpec(memory_space=pltpu.VMEM)
    hbm = pl.BlockSpec(memory_space=pltpu.HBM)
    dma = pltpu.SemaphoreType.DMA
    shapes = (
        jax.ShapeDtypeStruct((rows, cols), bf16),
        jax.ShapeDtypeStruct((rows, cols), bf16),
        jax.ShapeDtypeStruct((rows, D), bf16),
        jax.ShapeDtypeStruct((rows, D), bf16),
    )
    results = pl.pallas_call(
        functools.partial(kernel, n_seq, n_kvh),
        out_shape=tuple(pltpu.VMEM(shape.shape, shape.dtype) for shape in shapes),
        in_specs=[vmem, hbm, hbm, hbm, hbm],
        out_specs=(vmem, vmem, vmem, vmem),
        scratch_shapes=[
            pltpu.VMEM((rows, cols), bf16),
            pltpu.VMEM((rows, cols), bf16),
            pltpu.VMEM((chunks, D, wide), bf16),
            pltpu.VMEM((chunks, D, wide), bf16),
            pltpu.VMEM((WIN, 2, rows, D), bf16),
            pltpu.VMEM((WIN, D, rows), bf16),
            pltpu.VMEM((WIN, D + ONES, rows), bf16),
            pltpu.VMEM((WIN, rows, rows), f32),
            pltpu.VMEM((WIN, chunks, rows, wide), f32),
            pltpu.VMEM((WIN + 1, chunks, 1, wide), f32),
            pltpu.VMEM((chunks, D + ONES, wide), f32),
            pltpu.VMEM((chunks, D, wide), bf16),
            pltpu.VMEM((chunks, D, wide), f32),
            pltpu.VMEM((WIN, chunks, 1, wide), f32),
            pltpu.VMEM((chunks, 1, wide), f32),
            pltpu.VMEM((WIN, 2, D, rows), f32),
            pltpu.VMEM((SPAN, 2, D, rows), bf16),
            pltpu.VMEM((SPAN, 2, D, rows), bf16),
            dma((4,)),
            dma((4, n_kvh - 1)),
            dma((4, n_kvh - 1)),
            dma((SPAN, 2)),
            dma((SPAN, 2)),
            dma((SPAN, 2)),
            dma((SPAN, 2)),
        ],
        compiler_params=pltpu.CompilerParams(
            collective_id=0, has_side_effects=True, vmem_limit_bytes=48 * 1024 * 1024
        ),
    )(
        *(
            pltpu.with_memory_space_constraint(operand, pltpu.HBM)
            for operand in (doc_lengths.reshape(1, -1), query_in, key_in, value_in, grad_out)
        )
    )
    return pl.pallas_call(
        settle,
        out_shape=shapes,
        in_specs=[vmem] * len(shapes),
        out_specs=(hbm,) * len(shapes),
        scratch_shapes=[dma((len(shapes),))],
    )(*(pltpu.with_memory_space_constraint(result, pltpu.VMEM) for result in results))


def solution(mesh):
    placed = (
        P(("seq", "kvh"), None),
        P(("seq", "kvh"), None),
        P(("seq", "kvh"), None),
        P("seq", "kvh"),
        P(),
    )
    return jax.shard_map(
        functools.partial(per_device, mesh.shape["seq"], mesh.shape["kvh"]),
        mesh=mesh,
        in_specs=placed,
        out_specs=(P("seq", "kvh"), P("seq", "kvh"), P("seq", "kvh"), P("seq", "kvh")),
        check_vma=False,
    )
```

```python
import functools
import math

import jax
import jax.numpy as jnp
from jax import lax
from jax.experimental import pallas as pl
from jax.experimental.pallas import tpu as pltpu
from jax.sharding import PartitionSpec as P

MESH = pl.DeviceIdType.MESH
D = 128
SPAN = 3
WIN = SPAN + 1
HIDDEN = -1e30
SCALE = 1.0 / math.sqrt(D)
SCALE_2 = SCALE * math.log2(math.e)
PAIR = 2


def dot(a, b):
    return jnp.dot(a, b, preferred_element_type=jnp.float32)


def dot_nt(a, b):
    return lax.dot_general(a, b, (((1,), (1,)), ((), ())), preferred_element_type=jnp.float32)


def kernel(
    n_seq,
    n_kvh,
    doc_ref,
    q_hbm,
    k_hbm,
    v_hbm,
    do_hbm,
    attn_ref,
    dq_ref,
    dk_ref,
    dv_ref,
    q_loc,
    do_loc,
    q_t,
    do_t,
    kv,
    k_t,
    v_t,
    bias,
    prob_s,
    max_s,
    sum_s,
    out_t,
    attn_t,
    dq_t,
    ratio_s,
    delta_s,
    part,
    snd,
    rcv,
    local_sem,
    a2a_send,
    a2a_recv,
    halo_send,
    halo_recv,
    back_send,
    back_recv,
):
    rows, cols = do_loc.shape
    chunks, wide = q_t.shape[0], q_t.shape[2]
    pair = wide // rows
    per_half = chunks // 2
    piece = q_hbm.shape[0]
    s, g = lax.axis_index("seq"), lax.axis_index("kvh")
    nxt, prv = lax.rem(s + 1, n_seq), lax.rem(s + n_seq - 1, n_seq)

    def columns(h, width=D):
        return pl.ds(pl.multiple_of(h * width, width), width)

    mine = pl.ds(pl.multiple_of(g * piece, piece), piece)

    locals_ = [
        pltpu.make_async_copy(k_hbm.at[:, columns(g)], kv.at[SPAN, 0, mine, :], local_sem.at[0]),
        pltpu.make_async_copy(v_hbm.at[:, columns(g)], kv.at[SPAN, 1, mine, :], local_sem.at[1]),
        pltpu.make_async_copy(do_hbm, do_loc, local_sem.at[2]),
        pltpu.make_async_copy(q_hbm.at[:, columns(g, cols)], q_loc.at[mine, :], local_sem.at[3]),
    ]
    for copy in locals_:
        copy.start()

    barrier = pltpu.get_barrier_semaphore()
    for j in range(1, n_kvh):
        pl.semaphore_signal(
            barrier, inc=1, device_id=(s, lax.rem(g + j, n_kvh)), device_id_type=MESH
        )
    for to in (nxt, prv):
        pl.semaphore_signal(barrier, inc=1, device_id=(to, g), device_id_type=MESH)
    pl.semaphore_wait(barrier, n_kvh + 1)

    def to_peer(kind, j):
        peer = lax.rem(g + j, n_kvh)
        if kind >= 2:
            half = cols // 2
            src = q_hbm.at[:, columns(2 * peer + kind - 2, half)]
            dst = q_loc.at[mine, pl.ds((kind - 2) * half, half)]
        else:
            src = (k_hbm, v_hbm)[kind].at[:, columns(peer)]
            dst = kv.at[SPAN, kind, mine, :]
        return pltpu.make_async_remote_copy(
            src_ref=src,
            dst_ref=dst,
            send_sem=a2a_send.at[kind, j - 1],
            recv_sem=a2a_recv.at[kind, j - 1],
            device_id=(s, peer),
            device_id_type=MESH,
        )

    sends = [[to_peer(kind, j) for j in range(1, n_kvh)] for kind in range(4)]
    half_rows = rows // 2

    def halo(hop, kind, part_):
        place = (kind, pl.ds(part_ * half_rows, half_rows), slice(None))
        return pltpu.make_async_remote_copy(
            src_ref=kv.at[(SPAN - hop,) + place],
            dst_ref=kv.at[(SPAN - hop - 1,) + place],
            send_sem=halo_send.at[hop, kind, part_],
            recv_sem=halo_recv.at[hop, kind, part_],
            device_id=(nxt, g),
            device_id_type=MESH,
        )

    halos = [
        [[halo(hop, kind, part_) for part_ in range(2)] for kind in range(2)]
        for hop in range(SPAN)
    ]

    def back(hop, kind, part_):
        return pltpu.make_async_remote_copy(
            src_ref=snd.at[hop, kind, part_],
            dst_ref=rcv.at[hop, kind, part_],
            send_sem=back_send.at[hop, kind, part_],
            recv_sem=back_recv.at[hop, kind, part_],
            device_id=(prv, g),
            device_id_type=MESH,
        )

    backs = [
        [[back(hop, kind, part_) for part_ in range(2)] for kind in range(2)]
        for hop in range(SPAN)
    ]

    def set_mask():
        docs = doc_ref.shape[1]
        lens = jnp.broadcast_to(doc_ref[...].astype(jnp.float32), (docs, docs))
        upto = lax.broadcasted_iota(jnp.int32, (docs, docs), 1) <= lax.broadcasted_iota(
            jnp.int32, (docs, docs), 0
        )
        ends = jnp.sum(jnp.where(upto, lens, 0.0), axis=1, keepdims=True)
        q_pos = (s * rows + lax.broadcasted_iota(jnp.int32, (1, rows), 1)).astype(jnp.float32)
        begin = jnp.max(jnp.where(ends <= q_pos, ends, 0.0), axis=0, keepdims=True)

        def one_block(w, _):
            k_pos = (
                (s - SPAN + w) * rows + lax.broadcasted_iota(jnp.int32, (rows, rows), 0)
            ).astype(jnp.float32)
            seen = (k_pos >= begin) & (k_pos <= q_pos)
            bias[w] = jnp.where(seen, 0.0, HIDDEN)
            part[w] = jnp.zeros(part.shape[1:], jnp.float32)
            return 0

        lax.fori_loop(0, WIN, one_block, 0)

        def clear(c, _):
            max_s[WIN, c] = jnp.full(max_s.shape[2:], HIDDEN, jnp.float32)
            out_t[c] = jnp.zeros(out_t.shape[1:], jnp.float32)
            dq_t[c] = jnp.zeros(dq_t.shape[1:], jnp.float32)
            return 0

        lax.fori_loop(0, chunks, clear, 0)

    def turn(src, dst, c):
        for u in range(pair):
            dst[c, :, u * rows : (u + 1) * rows] = src[:, columns(c * pair + u)].T

    def take_queries(half):
        for copy in sends[2 + half]:
            copy.wait_recv()
        for c in range(half * per_half, (half + 1) * per_half):
            turn(q_loc, q_t, c)

    def piece_on(kind, j):
        source = lax.rem(g + n_kvh - j, n_kvh)
        part_ = source // (n_kvh // 2)
        place = (kind, pl.ds(pl.multiple_of(source * piece, piece), piece), slice(None))
        pltpu.make_async_remote_copy(
            src_ref=kv.at[(SPAN,) + place],
            dst_ref=kv.at[(SPAN - 1,) + place],
            send_sem=halo_send.at[0, kind, part_],
            recv_sem=halo_recv.at[0, kind, part_],
            device_id=(nxt, g),
            device_id_type=MESH,
        ).start()

    near_first = sorted(range(1, n_kvh), key=lambda j: min(j, n_kvh - j))

    def pieces_on(kind):
        for j in near_first:
            sends[kind][j - 1].wait_recv()
            piece_on(kind, j)

    def pass_on(hop, kind):
        for part_ in range(2):
            halos[hop - 1][kind][part_].wait_recv()
            if hop < SPAN:
                halos[hop][kind][part_].start()

    for copy in sends[0]:
        copy.start()
    locals_[0].wait()
    piece_on(0, 0)
    for kind in range(1, 4):
        for copy in sends[kind]:
            copy.start()
    set_mask()

    pieces_on(0)
    pass_on(1, 0)
    pass_on(2, 0)
    locals_[1].wait()
    piece_on(1, 0)
    pieces_on(1)

    locals_[2].wait()

    def turn_grad(c, _):
        turn(do_loc, do_t, c)
        return 0

    lax.fori_loop(0, chunks, turn_grad, 0)

    def turn_k(w, _):
        k_t[w] = kv[w, 0].T
        return 0

    lax.fori_loop(1, WIN, turn_k, 0)
    v_t[SPAN] = kv[SPAN, 1].T
    locals_[3].wait()
    take_queries(0)

    def chunks_of(half):
        return [half * per_half + c for c in range(per_half)]

    def weigh(step, _):
        early = 1 - step // 4
        w = SPAN - early * lax.rem(step, 2) - (1 - early) * (step // 2)
        half = early * (step // 2) + (1 - early) * lax.rem(step, 2)

        @pl.when(step == 2)
        def _():
            take_queries(1)

        @pl.when(step == 5)
        def _():
            pass_on(1, 1)

        @pl.when(step == 6)
        def _():
            pass_on(SPAN, 0)

        mask = jnp.concatenate([bias[w]] * pair, axis=1)
        scores = [dot(kv[w, 0], q_t[c]) + mask for c in chunks_of(half)]
        for c, score in zip(chunks_of(half), scores):
            top = jnp.maximum(jnp.max(score, axis=0, keepdims=True), max_s[w + 1, c])
            max_s[w, c] = top
            prob = jnp.exp2(score * SCALE_2 - top * SCALE_2)
            prob_s[w, c] = prob
            sum_s[w, c] = jnp.sum(prob, axis=0, keepdims=True)
        return 0

    lax.fori_loop(0, 2 * WIN, weigh, 0)

    def even_out(c, _):
        shares = [jnp.exp2((max_s[w, c] - max_s[0, c]) * SCALE_2) for w in range(WIN)]
        inv = 1.0 / sum(shares[w] * sum_s[w, c] for w in range(WIN))
        for w in range(WIN):
            ratio_s[w, c] = shares[w] * inv
        return 0

    lax.fori_loop(0, chunks, even_out, 0)

    def pass_back(hop, kind):
        for part_ in range(2):
            here = slice(part_ * half_rows, (part_ + 1) * half_rows)
            total = part[hop, kind, :, here]
            if kind == 0:
                total = total * SCALE
            if hop > 0:
                backs[hop - 1][kind][part_].wait_recv()
                total = total + rcv[hop - 1, kind, part_].astype(jnp.float32)
            total = total.astype(jnp.bfloat16)
            if hop < SPAN:
                snd[hop, kind, part_] = total
                backs[hop][kind][part_].start()
            else:
                (dk_ref, dv_ref)[kind][here, :] = total.T

    def prob_of(w, c):
        return prob_s[w, c] * ratio_s[w, c]

    def oldest_dv(half, _):
        for c in chunks_of(half):
            part[0, 1] += dot_nt(do_t[c], prob_of(0, c).astype(jnp.bfloat16))
        return 0

    lax.fori_loop(0, 2, oldest_dv, 0)
    pass_back(0, 1)
    pass_on(2, 1)
    for w in (2, 1):
        v_t[w] = kv[w, 1].T

    def values(step, _):
        w, half = step // 2, lax.rem(step, 2)
        for c in chunks_of(half):
            prob = prob_of(w, c).astype(jnp.bfloat16)
            part[w, 1] += dot_nt(do_t[c], prob)
            out_t[c] += dot(v_t[w], prob)

        @pl.when(step == 5)
        def _():
            pass_back(1, 1)

        return 0

    lax.fori_loop(2, 2 * WIN, values, 0)
    pass_on(SPAN, 1)
    v_t[0] = kv[0, 1].T
    k_t[0] = kv[0, 0].T

    def finish(half, _):
        for c in chunks_of(half):
            out = out_t[c] + dot(v_t[0], prob_of(0, c).astype(jnp.bfloat16))
            out = out.astype(jnp.bfloat16)
            attn_t[c] = out
            delta_s[c] = jnp.sum(
                out.astype(jnp.float32) * do_t[c].astype(jnp.float32), axis=0, keepdims=True
            )
        return 0

    lax.fori_loop(0, 2, finish, 0)

    def unturn(src, dst, scale):
        def one(c, _):
            for u in range(pair):
                part_ = src[c, :, u * rows : (u + 1) * rows]
                if scale is not None:
                    part_ = (part_ * scale).astype(jnp.bfloat16)
                dst[:, columns(c * pair + u)] = part_.T
            return 0

        lax.fori_loop(0, chunks, one, 0)

    def keys(step, _):
        w, half = step // 2, lax.rem(step, 2)
        grads = [dot(kv[w, 1], do_t[c]) for c in chunks_of(half)]
        for c, grad in zip(chunks_of(half), grads):
            ds = (prob_of(w, c) * (grad - delta_s[c])).astype(jnp.bfloat16)
            part[w, 0] += dot_nt(q_t[c], ds)
            dq_t[c] += dot(k_t[w], ds)

        @pl.when(step == 1)
        def _():
            pass_back(0, 0)
            pass_back(2, 1)

        @pl.when(step == 5)
        def _():
            pass_back(1, 0)

        return 0

    lax.fori_loop(0, 2 * WIN, keys, 0)
    unturn(attn_t, attn_ref, None)
    pass_back(2, 0)
    unturn(dq_t, dq_ref, SCALE)
    pass_back(SPAN, 1)
    pass_back(SPAN, 0)

    for group in sends + [kind for hop in halos + backs for kind in hop]:
        for copy in group:
            copy.wait_send()


def settle(*refs):
    n = len(refs) // 2
    copies = [
        pltpu.make_async_copy(refs[i], refs[n + i], refs[-1].at[i]) for i in range(n)
    ]
    for copy in copies:
        copy.start()
    for copy in copies:
        copy.wait()


def per_device(n_seq, n_kvh, query_in, key_in, value_in, grad_out, doc_lengths):
    rows, cols = grad_out.shape
    chunks, wide = cols // (D * PAIR), PAIR * rows
    bf16, f32 = jnp.bfloat16, jnp.float32
    vmem = pl.BlockSpec(memory_space=pltpu.VMEM)
    hbm = pl.BlockSpec(memory_space=pltpu.HBM)
    dma = pltpu.SemaphoreType.DMA
    shapes = (
        jax.ShapeDtypeStruct((rows, cols), bf16),
        jax.ShapeDtypeStruct((rows, cols), bf16),
        jax.ShapeDtypeStruct((rows, D), bf16),
        jax.ShapeDtypeStruct((rows, D), bf16),
    )
    results = pl.pallas_call(
        functools.partial(kernel, n_seq, n_kvh),
        out_shape=tuple(pltpu.VMEM(shape.shape, shape.dtype) for shape in shapes),
        in_specs=[vmem, hbm, hbm, hbm, hbm],
        out_specs=(vmem, vmem, vmem, vmem),
        scratch_shapes=[
            pltpu.VMEM((rows, cols), bf16),
            pltpu.VMEM((rows, cols), bf16),
            pltpu.VMEM((chunks, D, wide), bf16),
            pltpu.VMEM((chunks, D, wide), bf16),
            pltpu.VMEM((WIN, 2, rows, D), bf16),
            pltpu.VMEM((WIN, D, rows), bf16),
            pltpu.VMEM((WIN, D, rows), bf16),
            pltpu.VMEM((WIN, rows, rows), f32),
            pltpu.VMEM((WIN, chunks, rows, wide), f32),
            pltpu.VMEM((WIN + 1, chunks, 1, wide), f32),
            pltpu.VMEM((WIN, chunks, 1, wide), f32),
            pltpu.VMEM((chunks, D, wide), f32),
            pltpu.VMEM((chunks, D, wide), bf16),
            pltpu.VMEM((chunks, D, wide), f32),
            pltpu.VMEM((WIN, chunks, 1, wide), f32),
            pltpu.VMEM((chunks, 1, wide), f32),
            pltpu.VMEM((WIN, 2, D, rows), f32),
            pltpu.VMEM((SPAN, 2, 2, D, rows // 2), bf16),
            pltpu.VMEM((SPAN, 2, 2, D, rows // 2), bf16),
            dma((4,)),
            dma((4, n_kvh - 1)),
            dma((4, n_kvh - 1)),
            dma((SPAN, 2, 2)),
            dma((SPAN, 2, 2)),
            dma((SPAN, 2, 2)),
            dma((SPAN, 2, 2)),
        ],
        compiler_params=pltpu.CompilerParams(
            collective_id=0, has_side_effects=True, vmem_limit_bytes=48 * 1024 * 1024
        ),
    )(
        *(
            pltpu.with_memory_space_constraint(operand, pltpu.HBM)
            for operand in (doc_lengths.reshape(1, -1), query_in, key_in, value_in, grad_out)
        )
    )
    return pl.pallas_call(
        settle,
        out_shape=shapes,
        in_specs=[vmem] * len(shapes),
        out_specs=(hbm,) * len(shapes),
        scratch_shapes=[dma((len(shapes),))],
    )(*(pltpu.with_memory_space_constraint(result, pltpu.VMEM) for result in results))


def solution(mesh):
    placed = (
        P(("seq", "kvh"), None),
        P(("seq", "kvh"), None),
        P(("seq", "kvh"), None),
        P("seq", "kvh"),
        P(),
    )
    return jax.shard_map(
        functools.partial(per_device, mesh.shape["seq"], mesh.shape["kvh"]),
        mesh=mesh,
        in_specs=placed,
        out_specs=(P("seq", "kvh"), P("seq", "kvh"), P("seq", "kvh"), P("seq", "kvh")),
        check_vma=False,
    )
```

```python
import functools
import math

import jax
import jax.numpy as jnp
from jax import lax
from jax.experimental import pallas as pl
from jax.experimental.pallas import tpu as pltpu
from jax.sharding import PartitionSpec as P

MESH = pl.DeviceIdType.MESH
D = 128
SPAN = 3
WIN = SPAN + 1
ONES = 16
HIDDEN = -1e30
SCALE = 1.0 / math.sqrt(D)
SCALE_2 = SCALE * math.log2(math.e)
PAIR = 2


def dot(a, b):
    return jnp.dot(a, b, preferred_element_type=jnp.float32)


def dot_nt(a, b):
    return lax.dot_general(a, b, (((1,), (1,)), ((), ())), preferred_element_type=jnp.float32)


def kernel(
    n_seq,
    n_kvh,
    doc_ref,
    q_hbm,
    k_hbm,
    v_hbm,
    do_hbm,
    attn_ref,
    dq_ref,
    dk_ref,
    dv_ref,
    q_loc,
    do_loc,
    q_t,
    do_t,
    kv,
    k_t,
    v_t,
    bias,
    prob_s,
    max_s,
    out_t,
    attn_t,
    dq_t,
    ratio_s,
    delta_s,
    part,
    snd,
    rcv,
    local_sem,
    a2a_send,
    a2a_recv,
    halo_send,
    halo_recv,
    back_send,
    back_recv,
):
    rows, cols = do_loc.shape
    chunks, wide = q_t.shape[0], q_t.shape[2]
    pair = wide // rows
    per_half = chunks // 2
    piece = q_hbm.shape[0]
    s, g = lax.axis_index("seq"), lax.axis_index("kvh")
    nxt, prv = lax.rem(s + 1, n_seq), lax.rem(s + n_seq - 1, n_seq)

    def columns(h, width=D):
        return pl.ds(pl.multiple_of(h * width, width), width)

    mine = pl.ds(pl.multiple_of(g * piece, piece), piece)

    locals_ = [
        pltpu.make_async_copy(k_hbm.at[:, columns(g)], kv.at[SPAN, 0, mine, :], local_sem.at[0]),
        pltpu.make_async_copy(v_hbm.at[:, columns(g)], kv.at[SPAN, 1, mine, :], local_sem.at[1]),
        pltpu.make_async_copy(do_hbm, do_loc, local_sem.at[2]),
        pltpu.make_async_copy(q_hbm.at[:, columns(g, cols)], q_loc.at[mine, :], local_sem.at[3]),
    ]
    for copy in locals_:
        copy.start()

    barrier = pltpu.get_barrier_semaphore()
    for j in range(1, n_kvh):
        pl.semaphore_signal(
            barrier, inc=1, device_id=(s, lax.rem(g + j, n_kvh)), device_id_type=MESH
        )
    for to in (nxt, prv):
        pl.semaphore_signal(barrier, inc=1, device_id=(to, g), device_id_type=MESH)
    pl.semaphore_wait(barrier, n_kvh + 1)

    def to_peer(kind, j):
        peer = lax.rem(g + j, n_kvh)
        if kind >= 2:
            half = cols // 2
            src = q_hbm.at[:, columns(2 * peer + kind - 2, half)]
            dst = q_loc.at[mine, pl.ds((kind - 2) * half, half)]
        else:
            src = (k_hbm, v_hbm)[kind].at[:, columns(peer)]
            dst = kv.at[SPAN, kind, mine, :]
        return pltpu.make_async_remote_copy(
            src_ref=src,
            dst_ref=dst,
            send_sem=a2a_send.at[kind],
            recv_sem=a2a_recv.at[kind],
            device_id=(s, peer),
            device_id_type=MESH,
        )

    def send(kind):
        for j in range(1, n_kvh):
            to_peer(kind, j).start()

    def all_pieces(kind):
        size = (n_kvh - 1) * piece
        half = cols // 2
        if kind >= 2:
            place = q_loc.at[:size, pl.ds((kind - 2) * half, half)]
        else:
            place = kv.at[SPAN, kind, :size, :]
        return pltpu.make_async_remote_copy(
            src_ref=place,
            dst_ref=place,
            send_sem=a2a_send.at[kind],
            recv_sem=a2a_recv.at[kind],
            device_id=(s, lax.rem(g + 1, n_kvh)),
            device_id_type=MESH,
        )

    def halo(hop, kind):
        return pltpu.make_async_remote_copy(
            src_ref=kv.at[SPAN - hop, kind],
            dst_ref=kv.at[SPAN - hop - 1, kind],
            send_sem=halo_send.at[hop, kind],
            recv_sem=halo_recv.at[hop, kind],
            device_id=(nxt, g),
            device_id_type=MESH,
        )

    halos = [[halo(hop, kind) for kind in range(2)] for hop in range(SPAN)]

    def back(hop, kind):
        return pltpu.make_async_remote_copy(
            src_ref=snd.at[hop, kind],
            dst_ref=rcv.at[hop, kind],
            send_sem=back_send.at[hop, kind],
            recv_sem=back_recv.at[hop, kind],
            device_id=(prv, g),
            device_id_type=MESH,
        )

    backs = [[back(hop, kind) for kind in range(2)] for hop in range(SPAN)]

    def turn(src, dst, c):
        for u in range(pair):
            dst[c, :, u * rows : (u + 1) * rows] = src[:, columns(c * pair + u)].T

    def turn_kv(w):
        k_t[w] = kv[w, 0].T
        v_t[w, :D, :] = kv[w, 1].T

    def pass_on(hop, kind):
        halos[hop - 1][kind].wait_recv()
        halos[hop][kind].start()

    def take_queries(half):
        all_pieces(2 + half).wait_recv()
        for c in range(half * per_half, (half + 1) * per_half):
            turn(q_loc, q_t, c)

    def set_mask():
        docs = doc_ref.shape[1]
        lens = jnp.broadcast_to(doc_ref[...].astype(jnp.float32), (docs, docs))
        upto = lax.broadcasted_iota(jnp.int32, (docs, docs), 1) <= lax.broadcasted_iota(
            jnp.int32, (docs, docs), 0
        )
        ends = jnp.sum(jnp.where(upto, lens, 0.0), axis=1, keepdims=True)
        q_pos = (s * rows + lax.broadcasted_iota(jnp.int32, (1, rows), 1)).astype(jnp.float32)
        begin = jnp.max(jnp.where(ends <= q_pos, ends, 0.0), axis=0, keepdims=True)

        def set_up(w, _):
            k_pos = (
                (s - SPAN + w) * rows + lax.broadcasted_iota(jnp.int32, (rows, rows), 0)
            ).astype(jnp.float32)
            seen = (k_pos >= begin) & (k_pos <= q_pos)
            bias[w] = jnp.where(seen, 0.0, HIDDEN)
            v_t[w, D:, :] = jnp.ones((ONES, rows), jnp.bfloat16)
            part[w] = jnp.zeros(part.shape[1:], jnp.float32)
            return 0

        lax.fori_loop(0, WIN, set_up, 0)

        def clear(c, _):
            max_s[WIN, c] = jnp.full(max_s.shape[2:], HIDDEN, jnp.float32)
            out_t[c] = jnp.zeros(out_t.shape[1:], jnp.float32)
            dq_t[c] = jnp.zeros(dq_t.shape[1:], jnp.float32)
            return 0

        lax.fori_loop(0, chunks, clear, 0)

    def set_grad():
        locals_[2].wait()

        def one(c, _):
            turn(do_loc, do_t, c)
            return 0

        lax.fori_loop(0, chunks, one, 0)

    for kind in range(3):
        send(kind)
    set_mask()
    for kind in range(2):
        locals_[kind].wait()
        all_pieces(kind).wait_recv()
        halos[0][kind].start()
    send(3)
    set_grad()
    turn_kv(SPAN)
    pass_on(1, 0)
    pass_on(1, 1)
    turn_kv(SPAN - 1)
    pass_on(2, 0)
    locals_[3].wait()
    take_queries(0)

    def weigh(w, c, score):
        old = max_s[w + 1, c]
        top = jnp.maximum(jnp.max(score, axis=0, keepdims=True), old)
        max_s[w, c] = top
        prob = jnp.exp2(score * SCALE_2 - top * SCALE_2)
        prob_s[w, c] = prob
        return prob

    def gather(w, c, prob):
        shrink = jnp.exp2((max_s[w + 1, c] - max_s[w, c]) * SCALE_2)
        out_t[c] = out_t[c] * shrink + dot(v_t[w], prob.astype(jnp.bfloat16))

    def chunks_of(half):
        return [half * per_half + c for c in range(per_half)]

    def scores(w, half):
        mask = jnp.concatenate([bias[w]] * pair, axis=1)
        return [dot(kv[w, 0], q_t[c]) + mask for c in chunks_of(half)]

    def forward(step, _):
        early = 1 - step // 4
        w = SPAN - early * lax.rem(step, 2) - (1 - early) * 2
        half = early * (step // 2) + (1 - early) * lax.rem(step, 2)

        @pl.when(step == 1)
        def _():
            pass_on(2, 1)

        @pl.when(step == 2)
        def _():
            take_queries(1)

        @pl.when(step == 4)
        def _():
            turn_kv(1)

        for c, score in zip(chunks_of(half), scores(w, half)):
            gather(w, c, weigh(w, c, score))
        return 0

    lax.fori_loop(0, 6, forward, 0)

    def oldest_scores(half, _):
        for c, score in zip(chunks_of(half), scores(0, half)):
            weigh(0, c, score)
        return 0

    halos[2][0].wait_recv()
    lax.fori_loop(0, 2, oldest_scores, 0)
    halos[2][1].wait_recv()
    turn_kv(0)

    def oldest_sum(c, _):
        gather(0, c, prob_s[0, c])
        return 0

    lax.fori_loop(0, chunks, oldest_sum, 0)

    def finish(c, _):
        inv = 1.0 / out_t[c, D : D + 1, :]
        top = max_s[0, c]
        for w in range(WIN):
            ratio_s[w, c] = jnp.exp2((max_s[w, c] - top) * SCALE_2) * inv
        out = (out_t[c, :D, :] * inv).astype(jnp.bfloat16)
        attn_t[c] = out
        delta_s[c] = jnp.sum(
            out.astype(jnp.float32) * do_t[c].astype(jnp.float32), axis=0, keepdims=True
        )
        return 0

    lax.fori_loop(0, chunks, finish, 0)

    def pass_back(hop, kinds=(1, 0)):
        for kind in kinds:
            total = part[hop, kind] * SCALE if kind == 0 else part[hop, kind]
            if hop > 0:
                backs[hop - 1][kind].wait_recv()
                total = total + rcv[hop - 1, kind].astype(jnp.float32)
            if hop < SPAN:
                snd[hop, kind] = total.astype(jnp.bfloat16)
                backs[hop][kind].start()
            else:
                (dk_ref, dv_ref)[kind][...] = total.astype(jnp.bfloat16).T

    def unturn(src, dst, scale):
        def one(c, _):
            for u in range(pair):
                part_ = src[c, :, u * rows : (u + 1) * rows]
                if scale is not None:
                    part_ = (part_ * scale).astype(jnp.bfloat16)
                dst[:, columns(c * pair + u)] = part_.T
            return 0

        lax.fori_loop(0, chunks, one, 0)

    def one_dv(w, c, prob):
        part[w, 1] += dot_nt(do_t[c], prob.astype(jnp.bfloat16))

    def one_dk(w, c, prob, grad):
        ds = (prob * (grad - delta_s[c])).astype(jnp.bfloat16)
        part[w, 0] += dot_nt(q_t[c], ds)
        dq_t[c] += dot(k_t[w], ds)

    def oldest_dv(half, _):
        for c in chunks_of(half):
            one_dv(0, c, prob_s[0, c] * ratio_s[0, c])
        return 0

    def oldest_dk(half, _):
        grads = [dot(kv[0, 1], do_t[c]) for c in chunks_of(half)]
        for c, grad in zip(chunks_of(half), grads):
            one_dk(0, c, prob_s[0, c] * ratio_s[0, c], grad)
        return 0

    lax.fori_loop(0, 2, oldest_dv, 0)
    pass_back(0, (1,))
    lax.fori_loop(0, 2, oldest_dk, 0)
    pass_back(0, (0,))

    def backward(step, _):
        w, half = step // 2, lax.rem(step, 2)
        grads = [dot(kv[w, 1], do_t[c]) for c in chunks_of(half)]
        for c, grad in zip(chunks_of(half), grads):
            prob = prob_s[w, c] * ratio_s[w, c]
            one_dv(w, c, prob)
            one_dk(w, c, prob, grad)

        for hop in range(1, SPAN):

            @pl.when(step == 2 * hop + 1)
            def _(hop=hop):
                if hop == 1:
                    unturn(attn_t, attn_ref, None)
                pass_back(hop)

        return 0

    lax.fori_loop(2, 2 * WIN, backward, 0)
    unturn(dq_t, dq_ref, SCALE)
    pass_back(SPAN)

    for kind in range(4):
        all_pieces(kind).wait_send()
    for group in halos + backs:
        for copy in group:
            copy.wait_send()


def settle(*refs):
    n = len(refs) // 2
    copies = [
        pltpu.make_async_copy(refs[i], refs[n + i], refs[-1].at[i]) for i in range(n)
    ]
    for copy in copies:
        copy.start()
    for copy in copies:
        copy.wait()


def per_device(n_seq, n_kvh, query_in, key_in, value_in, grad_out, doc_lengths):
    rows, cols = grad_out.shape
    chunks, wide = cols // (D * PAIR), PAIR * rows
    bf16, f32 = jnp.bfloat16, jnp.float32
    vmem = pl.BlockSpec(memory_space=pltpu.VMEM)
    hbm = pl.BlockSpec(memory_space=pltpu.HBM)
    dma = pltpu.SemaphoreType.DMA
    shapes = (
        jax.ShapeDtypeStruct((rows, cols), bf16),
        jax.ShapeDtypeStruct((rows, cols), bf16),
        jax.ShapeDtypeStruct((rows, D), bf16),
        jax.ShapeDtypeStruct((rows, D), bf16),
    )
    results = pl.pallas_call(
        functools.partial(kernel, n_seq, n_kvh),
        out_shape=tuple(pltpu.VMEM(shape.shape, shape.dtype) for shape in shapes),
        in_specs=[vmem, hbm, hbm, hbm, hbm],
        out_specs=(vmem, vmem, vmem, vmem),
        scratch_shapes=[
            pltpu.VMEM((rows, cols), bf16),
            pltpu.VMEM((rows, cols), bf16),
            pltpu.VMEM((chunks, D, wide), bf16),
            pltpu.VMEM((chunks, D, wide), bf16),
            pltpu.VMEM((WIN, 2, rows, D), bf16),
            pltpu.VMEM((WIN, D, rows), bf16),
            pltpu.VMEM((WIN, D + ONES, rows), bf16),
            pltpu.VMEM((WIN, rows, rows), f32),
            pltpu.VMEM((WIN, chunks, rows, wide), f32),
            pltpu.VMEM((WIN + 1, chunks, 1, wide), f32),
            pltpu.VMEM((chunks, D + ONES, wide), f32),
            pltpu.VMEM((chunks, D, wide), bf16),
            pltpu.VMEM((chunks, D, wide), f32),
            pltpu.VMEM((WIN, chunks, 1, wide), f32),
            pltpu.VMEM((chunks, 1, wide), f32),
            pltpu.VMEM((WIN, 2, D, rows), f32),
            pltpu.VMEM((SPAN, 2, D, rows), bf16),
            pltpu.VMEM((SPAN, 2, D, rows), bf16),
            dma((4,)),
            dma((4,)),
            dma((4,)),
            dma((SPAN, 2)),
            dma((SPAN, 2)),
            dma((SPAN, 2)),
            dma((SPAN, 2)),
        ],
        compiler_params=pltpu.CompilerParams(
            collective_id=0, has_side_effects=True, vmem_limit_bytes=48 * 1024 * 1024
        ),
    )(
        *(
            pltpu.with_memory_space_constraint(operand, pltpu.HBM)
            for operand in (doc_lengths.reshape(1, -1), query_in, key_in, value_in, grad_out)
        )
    )
    return pl.pallas_call(
        settle,
        out_shape=shapes,
        in_specs=[vmem] * len(shapes),
        out_specs=(hbm,) * len(shapes),
        scratch_shapes=[dma((len(shapes),))],
    )(*(pltpu.with_memory_space_constraint(result, pltpu.VMEM) for result in results))


def solution(mesh):
    placed = (
        P(("seq", "kvh"), None),
        P(("seq", "kvh"), None),
        P(("seq", "kvh"), None),
        P("seq", "kvh"),
        P(),
    )
    return jax.shard_map(
        functools.partial(per_device, mesh.shape["seq"], mesh.shape["kvh"]),
        mesh=mesh,
        in_specs=placed,
        out_specs=(P("seq", "kvh"), P("seq", "kvh"), P("seq", "kvh"), P("seq", "kvh")),
        check_vma=False,
    )
```

```python
import functools
import math

import jax
import jax.numpy as jnp
from jax import lax
from jax.experimental import pallas as pl
from jax.experimental.pallas import tpu as pltpu
from jax.sharding import PartitionSpec as P

MESH = pl.DeviceIdType.MESH
D = 128
SPAN = 3
WIN = SPAN + 1
ONES = 16
HIDDEN = -1e30
SCALE = 1.0 / math.sqrt(D)
SCALE_2 = SCALE * math.log2(math.e)
PAIR = 4


def dot(a, b):
    return jnp.dot(a, b, preferred_element_type=jnp.float32)


def dot_nt(a, b):
    return lax.dot_general(a, b, (((1,), (1,)), ((), ())), preferred_element_type=jnp.float32)


def kernel(
    n_seq,
    n_kvh,
    doc_ref,
    q_hbm,
    k_hbm,
    v_hbm,
    do_hbm,
    attn_ref,
    dq_ref,
    dk_ref,
    dv_ref,
    q_loc,
    do_loc,
    q_t,
    do_t,
    kv,
    k_t,
    v_t,
    bias,
    prob_s,
    max_s,
    out_t,
    attn_t,
    dq_t,
    ratio_s,
    delta_s,
    part,
    snd,
    rcv,
    local_sem,
    a2a_send,
    a2a_recv,
    halo_send,
    halo_recv,
    back_send,
    back_recv,
):
    rows, cols = do_loc.shape
    chunks, wide = q_t.shape[0], q_t.shape[2]
    pair = wide // rows
    per_half = chunks // 2
    piece = q_hbm.shape[0]
    s, g = lax.axis_index("seq"), lax.axis_index("kvh")
    nxt, prv = lax.rem(s + 1, n_seq), lax.rem(s + n_seq - 1, n_seq)

    def columns(h, width=D):
        return pl.ds(pl.multiple_of(h * width, width), width)

    mine = pl.ds(pl.multiple_of(g * piece, piece), piece)

    locals_ = [
        pltpu.make_async_copy(k_hbm.at[:, columns(g)], kv.at[SPAN, 0, mine, :], local_sem.at[0]),
        pltpu.make_async_copy(v_hbm.at[:, columns(g)], kv.at[SPAN, 1, mine, :], local_sem.at[1]),
        pltpu.make_async_copy(do_hbm, do_loc, local_sem.at[2]),
        pltpu.make_async_copy(q_hbm.at[:, columns(g, cols)], q_loc.at[mine, :], local_sem.at[3]),
    ]
    for copy in locals_:
        copy.start()

    barrier = pltpu.get_barrier_semaphore()
    for j in range(1, n_kvh):
        pl.semaphore_signal(
            barrier, inc=1, device_id=(s, lax.rem(g + j, n_kvh)), device_id_type=MESH
        )
    for to in (nxt, prv):
        pl.semaphore_signal(barrier, inc=1, device_id=(to, g), device_id_type=MESH)
    pl.semaphore_wait(barrier, n_kvh + 1)

    def to_peer(kind, j):
        peer = lax.rem(g + j, n_kvh)
        if kind >= 2:
            half = cols // 2
            src = q_hbm.at[:, columns(2 * peer + kind - 2, half)]
            dst = q_loc.at[mine, pl.ds((kind - 2) * half, half)]
        else:
            src = (k_hbm, v_hbm)[kind].at[:, columns(peer)]
            dst = kv.at[SPAN, kind, mine, :]
        return pltpu.make_async_remote_copy(
            src_ref=src,
            dst_ref=dst,
            send_sem=a2a_send.at[kind],
            recv_sem=a2a_recv.at[kind],
            device_id=(s, peer),
            device_id_type=MESH,
        )

    def send(kind):
        for j in range(1, n_kvh):
            to_peer(kind, j).start()

    def all_pieces(kind):
        size = (n_kvh - 1) * piece
        half = cols // 2
        if kind >= 2:
            place = q_loc.at[:size, pl.ds((kind - 2) * half, half)]
        else:
            place = kv.at[SPAN, kind, :size, :]
        return pltpu.make_async_remote_copy(
            src_ref=place,
            dst_ref=place,
            send_sem=a2a_send.at[kind],
            recv_sem=a2a_recv.at[kind],
            device_id=(s, lax.rem(g + 1, n_kvh)),
            device_id_type=MESH,
        )

    def halo(hop, kind):
        return pltpu.make_async_remote_copy(
            src_ref=kv.at[SPAN - hop, kind],
            dst_ref=kv.at[SPAN - hop - 1, kind],
            send_sem=halo_send.at[hop, kind],
            recv_sem=halo_recv.at[hop, kind],
            device_id=(nxt, g),
            device_id_type=MESH,
        )

    halos = [[halo(hop, kind) for kind in range(2)] for hop in range(SPAN)]

    def back(hop, kind):
        return pltpu.make_async_remote_copy(
            src_ref=snd.at[hop, kind],
            dst_ref=rcv.at[hop, kind],
            send_sem=back_send.at[hop, kind],
            recv_sem=back_recv.at[hop, kind],
            device_id=(prv, g),
            device_id_type=MESH,
        )

    backs = [[back(hop, kind) for kind in range(2)] for hop in range(SPAN)]

    def turn(src, dst, c):
        for u in range(pair):
            dst[c, :, u * rows : (u + 1) * rows] = src[:, columns(c * pair + u)].T

    def turn_kv(w):
        k_t[w] = kv[w, 0].T
        v_t[w, :D, :] = kv[w, 1].T

    def pass_on(hop, kind):
        halos[hop - 1][kind].wait_recv()
        halos[hop][kind].start()

    def take_queries(half):
        all_pieces(2 + half).wait_recv()
        for c in range(half * per_half, (half + 1) * per_half):
            turn(q_loc, q_t, c)

    def set_mask():
        docs = doc_ref.shape[1]
        lens = jnp.broadcast_to(doc_ref[...].astype(jnp.float32), (docs, docs))
        upto = lax.broadcasted_iota(jnp.int32, (docs, docs), 1) <= lax.broadcasted_iota(
            jnp.int32, (docs, docs), 0
        )
        ends = jnp.sum(jnp.where(upto, lens, 0.0), axis=1, keepdims=True)
        q_pos = (s * rows + lax.broadcasted_iota(jnp.int32, (1, rows), 1)).astype(jnp.float32)
        begin = jnp.max(jnp.where(ends <= q_pos, ends, 0.0), axis=0, keepdims=True)

        def set_up(w, _):
            k_pos = (
                (s - SPAN + w) * rows + lax.broadcasted_iota(jnp.int32, (rows, rows), 0)
            ).astype(jnp.float32)
            seen = (k_pos >= begin) & (k_pos <= q_pos)
            bias[w] = jnp.where(seen, 0.0, HIDDEN)
            v_t[w, D:, :] = jnp.ones((ONES, rows), jnp.bfloat16)
            part[w] = jnp.zeros(part.shape[1:], jnp.float32)
            return 0

        lax.fori_loop(0, WIN, set_up, 0)

        def clear(c, _):
            max_s[WIN, c] = jnp.full(max_s.shape[2:], HIDDEN, jnp.float32)
            out_t[c] = jnp.zeros(out_t.shape[1:], jnp.float32)
            dq_t[c] = jnp.zeros(dq_t.shape[1:], jnp.float32)
            return 0

        lax.fori_loop(0, chunks, clear, 0)

    def set_grad():
        locals_[2].wait()

        def one(c, _):
            turn(do_loc, do_t, c)
            return 0

        lax.fori_loop(0, chunks, one, 0)

    for kind in range(3):
        send(kind)
    set_mask()
    for kind in range(2):
        locals_[kind].wait()
        all_pieces(kind).wait_recv()
        halos[0][kind].start()
    send(3)
    set_grad()
    turn_kv(SPAN)
    pass_on(1, 0)
    pass_on(1, 1)
    turn_kv(SPAN - 1)
    pass_on(2, 0)
    locals_[3].wait()
    take_queries(0)

    def weigh(w, c, score):
        old = max_s[w + 1, c]
        top = jnp.maximum(jnp.max(score, axis=0, keepdims=True), old)
        max_s[w, c] = top
        prob = jnp.exp2(score * SCALE_2 - top * SCALE_2)
        prob_s[w, c] = prob
        return prob

    def gather(w, c, prob):
        shrink = jnp.exp2((max_s[w + 1, c] - max_s[w, c]) * SCALE_2)
        out_t[c] = out_t[c] * shrink + dot(v_t[w], prob.astype(jnp.bfloat16))

    def chunks_of(half):
        return [half * per_half + c for c in range(per_half)]

    def scores(w, half):
        mask = jnp.concatenate([bias[w]] * pair, axis=1)
        return [dot(kv[w, 0], q_t[c]) + mask for c in chunks_of(half)]

    def forward(step, _):
        early = 1 - step // 4
        w = SPAN - early * lax.rem(step, 2) - (1 - early) * 2
        half = early * (step // 2) + (1 - early) * lax.rem(step, 2)

        @pl.when(step == 1)
        def _():
            pass_on(2, 1)

        @pl.when(step == 2)
        def _():
            take_queries(1)

        @pl.when(step == 4)
        def _():
            turn_kv(1)

        for c, score in zip(chunks_of(half), scores(w, half)):
            gather(w, c, weigh(w, c, score))
        return 0

    lax.fori_loop(0, 6, forward, 0)

    def oldest_scores(half, _):
        for c, score in zip(chunks_of(half), scores(0, half)):
            weigh(0, c, score)
        return 0

    halos[2][0].wait_recv()
    lax.fori_loop(0, 2, oldest_scores, 0)
    halos[2][1].wait_recv()
    turn_kv(0)

    def oldest_sum(c, _):
        gather(0, c, prob_s[0, c])
        return 0

    lax.fori_loop(0, chunks, oldest_sum, 0)

    def finish(c, _):
        inv = 1.0 / out_t[c, D : D + 1, :]
        top = max_s[0, c]
        for w in range(WIN):
            ratio_s[w, c] = jnp.exp2((max_s[w, c] - top) * SCALE_2) * inv
        out = (out_t[c, :D, :] * inv).astype(jnp.bfloat16)
        attn_t[c] = out
        delta_s[c] = jnp.sum(
            out.astype(jnp.float32) * do_t[c].astype(jnp.float32), axis=0, keepdims=True
        )
        return 0

    lax.fori_loop(0, chunks, finish, 0)

    def pass_back(hop, kinds=(1, 0)):
        for kind in kinds:
            total = part[hop, kind] * SCALE if kind == 0 else part[hop, kind]
            if hop > 0:
                backs[hop - 1][kind].wait_recv()
                total = total + rcv[hop - 1, kind].astype(jnp.float32)
            if hop < SPAN:
                snd[hop, kind] = total.astype(jnp.bfloat16)
                backs[hop][kind].start()
            else:
                (dk_ref, dv_ref)[kind][...] = total.astype(jnp.bfloat16).T

    def unturn(src, dst, scale):
        def one(c, _):
            for u in range(pair):
                part_ = src[c, :, u * rows : (u + 1) * rows]
                if scale is not None:
                    part_ = (part_ * scale).astype(jnp.bfloat16)
                dst[:, columns(c * pair + u)] = part_.T
            return 0

        lax.fori_loop(0, chunks, one, 0)

    def one_dv(w, c, prob):
        part[w, 1] += dot_nt(do_t[c], prob.astype(jnp.bfloat16))

    def one_dk(w, c, prob, grad):
        ds = (prob * (grad - delta_s[c])).astype(jnp.bfloat16)
        part[w, 0] += dot_nt(q_t[c], ds)
        dq_t[c] += dot(k_t[w], ds)

    def oldest_dv(half, _):
        for c in chunks_of(half):
            one_dv(0, c, prob_s[0, c] * ratio_s[0, c])
        return 0

    def oldest_dk(half, _):
        grads = [dot(kv[0, 1], do_t[c]) for c in chunks_of(half)]
        for c, grad in zip(chunks_of(half), grads):
            one_dk(0, c, prob_s[0, c] * ratio_s[0, c], grad)
        return 0

    lax.fori_loop(0, 2, oldest_dv, 0)
    pass_back(0, (1,))
    lax.fori_loop(0, 2, oldest_dk, 0)
    pass_back(0, (0,))

    def backward(step, _):
        w, half = step // 2, lax.rem(step, 2)
        grads = [dot(kv[w, 1], do_t[c]) for c in chunks_of(half)]
        for c, grad in zip(chunks_of(half), grads):
            prob = prob_s[w, c] * ratio_s[w, c]
            one_dv(w, c, prob)
            one_dk(w, c, prob, grad)

        for hop in range(1, SPAN):

            @pl.when(step == 2 * hop + 1)
            def _(hop=hop):
                if hop == 1:
                    unturn(attn_t, attn_ref, None)
                pass_back(hop)

        return 0

    lax.fori_loop(2, 2 * WIN, backward, 0)
    unturn(dq_t, dq_ref, SCALE)
    pass_back(SPAN)

    for kind in range(4):
        all_pieces(kind).wait_send()
    for group in halos + backs:
        for copy in group:
            copy.wait_send()


def settle(*refs):
    n = len(refs) // 2
    copies = [
        pltpu.make_async_copy(refs[i], refs[n + i], refs[-1].at[i]) for i in range(n)
    ]
    for copy in copies:
        copy.start()
    for copy in copies:
        copy.wait()


def per_device(n_seq, n_kvh, query_in, key_in, value_in, grad_out, doc_lengths):
    rows, cols = grad_out.shape
    chunks, wide = cols // (D * PAIR), PAIR * rows
    bf16, f32 = jnp.bfloat16, jnp.float32
    vmem = pl.BlockSpec(memory_space=pltpu.VMEM)
    hbm = pl.BlockSpec(memory_space=pltpu.HBM)
    dma = pltpu.SemaphoreType.DMA
    shapes = (
        jax.ShapeDtypeStruct((rows, cols), bf16),
        jax.ShapeDtypeStruct((rows, cols), bf16),
        jax.ShapeDtypeStruct((rows, D), bf16),
        jax.ShapeDtypeStruct((rows, D), bf16),
    )
    results = pl.pallas_call(
        functools.partial(kernel, n_seq, n_kvh),
        out_shape=tuple(pltpu.VMEM(shape.shape, shape.dtype) for shape in shapes),
        in_specs=[vmem, hbm, hbm, hbm, hbm],
        out_specs=(vmem, vmem, vmem, vmem),
        scratch_shapes=[
            pltpu.VMEM((rows, cols), bf16),
            pltpu.VMEM((rows, cols), bf16),
            pltpu.VMEM((chunks, D, wide), bf16),
            pltpu.VMEM((chunks, D, wide), bf16),
            pltpu.VMEM((WIN, 2, rows, D), bf16),
            pltpu.VMEM((WIN, D, rows), bf16),
            pltpu.VMEM((WIN, D + ONES, rows), bf16),
            pltpu.VMEM((WIN, rows, rows), f32),
            pltpu.VMEM((WIN, chunks, rows, wide), f32),
            pltpu.VMEM((WIN + 1, chunks, 1, wide), f32),
            pltpu.VMEM((chunks, D + ONES, wide), f32),
            pltpu.VMEM((chunks, D, wide), bf16),
            pltpu.VMEM((chunks, D, wide), f32),
            pltpu.VMEM((WIN, chunks, 1, wide), f32),
            pltpu.VMEM((chunks, 1, wide), f32),
            pltpu.VMEM((WIN, 2, D, rows), f32),
            pltpu.VMEM((SPAN, 2, D, rows), bf16),
            pltpu.VMEM((SPAN, 2, D, rows), bf16),
            dma((4,)),
            dma((4,)),
            dma((4,)),
            dma((SPAN, 2)),
            dma((SPAN, 2)),
            dma((SPAN, 2)),
            dma((SPAN, 2)),
        ],
        compiler_params=pltpu.CompilerParams(
            collective_id=0, has_side_effects=True, vmem_limit_bytes=48 * 1024 * 1024
        ),
    )(
        *(
            pltpu.with_memory_space_constraint(operand, pltpu.HBM)
            for operand in (doc_lengths.reshape(1, -1), query_in, key_in, value_in, grad_out)
        )
    )
    return pl.pallas_call(
        settle,
        out_shape=shapes,
        in_specs=[vmem] * len(shapes),
        out_specs=(hbm,) * len(shapes),
        scratch_shapes=[dma((len(shapes),))],
    )(*(pltpu.with_memory_space_constraint(result, pltpu.VMEM) for result in results))


def solution(mesh):
    placed = (
        P(("seq", "kvh"), None),
        P(("seq", "kvh"), None),
        P(("seq", "kvh"), None),
        P("seq", "kvh"),
        P(),
    )
    return jax.shard_map(
        functools.partial(per_device, mesh.shape["seq"], mesh.shape["kvh"]),
        mesh=mesh,
        in_specs=placed,
        out_specs=(P("seq", "kvh"), P("seq", "kvh"), P("seq", "kvh"), P("seq", "kvh")),
        check_vma=False,
    )
```

```python
import functools
import math

import jax
import jax.numpy as jnp
from jax import lax
from jax.experimental import pallas as pl
from jax.experimental.pallas import tpu as pltpu
from jax.sharding import PartitionSpec as P

MESH = pl.DeviceIdType.MESH
D = 128
SPAN = 3
WIN = SPAN + 1
ONES = 16
HIDDEN = -1e30
SCALE = 1.0 / math.sqrt(D)
SCALE_2 = SCALE * math.log2(math.e)
PAIR = 2


def dot(a, b):
    return jnp.dot(a, b, preferred_element_type=jnp.float32)


def dot_nt(a, b):
    return lax.dot_general(a, b, (((1,), (1,)), ((), ())), preferred_element_type=jnp.float32)


def kernel(
    n_seq,
    n_kvh,
    doc_ref,
    q_hbm,
    k_hbm,
    v_hbm,
    do_hbm,
    attn_ref,
    dq_ref,
    dk_ref,
    dv_ref,
    q_loc,
    do_loc,
    q_t,
    do_t,
    kv,
    k_t,
    v_t,
    bias,
    prob_s,
    max_s,
    out_t,
    attn_t,
    dq_t,
    ratio_s,
    delta_s,
    part,
    snd,
    rcv,
    local_sem,
    a2a_send,
    a2a_recv,
    halo_send,
    halo_recv,
    back_send,
    back_recv,
):
    rows, cols = do_loc.shape
    chunks, wide = q_t.shape[0], q_t.shape[2]
    pair = wide // rows
    per_half = chunks // 2
    piece = q_hbm.shape[0]
    s, g = lax.axis_index("seq"), lax.axis_index("kvh")
    nxt, prv = lax.rem(s + 1, n_seq), lax.rem(s + n_seq - 1, n_seq)

    def columns(h, width=D):
        return pl.ds(pl.multiple_of(h * width, width), width)

    mine = pl.ds(pl.multiple_of(g * piece, piece), piece)

    locals_ = [
        pltpu.make_async_copy(k_hbm.at[:, columns(g)], kv.at[SPAN, 0, mine, :], local_sem.at[0]),
        pltpu.make_async_copy(v_hbm.at[:, columns(g)], kv.at[SPAN, 1, mine, :], local_sem.at[1]),
        pltpu.make_async_copy(do_hbm, do_loc, local_sem.at[2]),
        pltpu.make_async_copy(q_hbm.at[:, columns(g, cols)], q_loc.at[mine, :], local_sem.at[3]),
    ]
    for copy in locals_:
        copy.start()

    barrier = pltpu.get_barrier_semaphore()
    for j in range(1, n_kvh):
        pl.semaphore_signal(
            barrier, inc=1, device_id=(s, lax.rem(g + j, n_kvh)), device_id_type=MESH
        )
    for to in (nxt, prv):
        pl.semaphore_signal(barrier, inc=1, device_id=(to, g), device_id_type=MESH)
    pl.semaphore_wait(barrier, n_kvh + 1)

    def to_peer(kind, j):
        peer = lax.rem(g + j, n_kvh)
        if kind >= 2:
            half = cols // 2
            src = q_hbm.at[:, columns(2 * peer + kind - 2, half)]
            dst = q_loc.at[mine, pl.ds((kind - 2) * half, half)]
        else:
            src = (k_hbm, v_hbm)[kind].at[:, columns(peer)]
            dst = kv.at[SPAN, kind, mine, :]
        return pltpu.make_async_remote_copy(
            src_ref=src,
            dst_ref=dst,
            send_sem=a2a_send.at[kind, j - 1],
            recv_sem=a2a_recv.at[kind, j - 1],
            device_id=(s, peer),
            device_id_type=MESH,
        )

    sends = [[to_peer(kind, j) for j in range(1, n_kvh)] for kind in range(4)]

    def start(copies):
        for copy in copies:
            copy.start()

    def halo(hop, kind):
        return pltpu.make_async_remote_copy(
            src_ref=kv.at[SPAN - hop, kind],
            dst_ref=kv.at[SPAN - hop - 1, kind],
            send_sem=halo_send.at[hop, kind],
            recv_sem=halo_recv.at[hop, kind],
            device_id=(nxt, g),
            device_id_type=MESH,
        )

    halos = [[halo(hop, kind) for kind in range(2)] for hop in range(SPAN)]

    def back(hop, kind):
        return pltpu.make_async_remote_copy(
            src_ref=snd.at[hop, kind],
            dst_ref=rcv.at[hop, kind],
            send_sem=back_send.at[hop, kind],
            recv_sem=back_recv.at[hop, kind],
            device_id=(prv, g),
            device_id_type=MESH,
        )

    backs = [[back(hop, kind) for kind in range(2)] for hop in range(SPAN)]

    def turn(src, dst, c):
        for u in range(pair):
            dst[c, :, u * rows : (u + 1) * rows] = src[:, columns(c * pair + u)].T

    def turn_kv(w):
        k_t[w] = kv[w, 0].T
        v_t[w, :D, :] = kv[w, 1].T

    def pass_on(hop, kind):
        halos[hop - 1][kind].wait_recv()
        halos[hop][kind].start()

    def take_queries(half):
        for copy in sends[2 + half]:
            copy.wait_recv()
        for c in range(half * per_half, (half + 1) * per_half):
            turn(q_loc, q_t, c)

    def set_all():
        docs = doc_ref.shape[1]
        lens = jnp.broadcast_to(doc_ref[...].astype(jnp.float32), (docs, docs))
        upto = lax.broadcasted_iota(jnp.int32, (docs, docs), 1) <= lax.broadcasted_iota(
            jnp.int32, (docs, docs), 0
        )
        ends = jnp.sum(jnp.where(upto, lens, 0.0), axis=1, keepdims=True)
        q_pos = (s * rows + lax.broadcasted_iota(jnp.int32, (1, rows), 1)).astype(jnp.float32)
        begin = jnp.max(jnp.where(ends <= q_pos, ends, 0.0), axis=0, keepdims=True)

        def set_up(w, _):
            k_pos = (
                (s - SPAN + w) * rows + lax.broadcasted_iota(jnp.int32, (rows, rows), 0)
            ).astype(jnp.float32)
            seen = (k_pos >= begin) & (k_pos <= q_pos)
            bias[w] = jnp.where(seen, 0.0, HIDDEN)
            v_t[w, D:, :] = jnp.ones((ONES, rows), jnp.bfloat16)
            part[w] = jnp.zeros(part.shape[1:], jnp.float32)
            return 0

        lax.fori_loop(0, WIN, set_up, 0)

        def clear(c, _):
            max_s[WIN, c] = jnp.full(max_s.shape[2:], HIDDEN, jnp.float32)
            out_t[c] = jnp.zeros(out_t.shape[1:], jnp.float32)
            dq_t[c] = jnp.zeros(dq_t.shape[1:], jnp.float32)
            return 0

        lax.fori_loop(0, chunks, clear, 0)

        locals_[2].wait()

        def set_grad(c, _):
            turn(do_loc, do_t, c)
            return 0

        lax.fori_loop(0, chunks, set_grad, 0)

    def piece_on(kind, j):
        place = (
            pl.ds(pl.multiple_of(lax.rem(g + n_kvh - j, n_kvh) * piece, piece), piece),
            slice(None),
        )
        pltpu.make_async_remote_copy(
            src_ref=kv.at[(SPAN, kind) + place],
            dst_ref=kv.at[(SPAN - 1, kind) + place],
            send_sem=halo_send.at[0, kind],
            recv_sem=halo_recv.at[0, kind],
            device_id=(nxt, g),
            device_id_type=MESH,
        ).start()

    near_first = sorted(range(1, n_kvh), key=lambda j: min(j, n_kvh - j))
    for kind in range(2):
        start(sends[kind])
    for kind in range(2):
        locals_[kind].wait()
        piece_on(kind, 0)
    for kind in range(2):
        for j in near_first:
            sends[kind][j - 1].wait_recv()
            piece_on(kind, j)
        start(sends[2 + kind])

    set_all()
    turn_kv(SPAN)
    pass_on(1, 0)
    pass_on(1, 1)
    turn_kv(SPAN - 1)
    pass_on(2, 0)
    locals_[3].wait()
    take_queries(0)

    def weigh(w, c, score):
        old = max_s[w + 1, c]
        top = jnp.maximum(jnp.max(score, axis=0, keepdims=True), old)
        max_s[w, c] = top
        prob = jnp.exp2(score * SCALE_2 - top * SCALE_2)
        prob_s[w, c] = prob
        return prob

    def gather(w, c, prob):
        shrink = jnp.exp2((max_s[w + 1, c] - max_s[w, c]) * SCALE_2)
        out_t[c] = out_t[c] * shrink + dot(v_t[w], prob.astype(jnp.bfloat16))

    def chunks_of(half):
        return [half * per_half + c for c in range(per_half)]

    def scores(w, half):
        mask = jnp.concatenate([bias[w]] * pair, axis=1)
        return [dot(kv[w, 0], q_t[c]) + mask for c in chunks_of(half)]

    def forward(step, _):
        early = 1 - step // 4
        w = SPAN - early * lax.rem(step, 2) - (1 - early) * 2
        half = early * (step // 2) + (1 - early) * lax.rem(step, 2)

        @pl.when(step == 1)
        def _():
            pass_on(2, 1)

        @pl.when(step == 2)
        def _():
            take_queries(1)

        @pl.when(step == 4)
        def _():
            turn_kv(1)

        for c, score in zip(chunks_of(half), scores(w, half)):
            gather(w, c, weigh(w, c, score))
        return 0

    lax.fori_loop(0, 6, forward, 0)

    def oldest_scores(half, _):
        for c, score in zip(chunks_of(half), scores(0, half)):
            prob = weigh(0, c, score)
            top = max_s[0, c]
            shares = [jnp.exp2((max_s[w, c] - top) * SCALE_2) for w in range(1, WIN)]
            before = out_t[c, D : D + 1, :] * shares[0]
            inv = 1.0 / (before + jnp.sum(prob, axis=0, keepdims=True))
            ratio_s[0, c] = inv
            for w in range(1, WIN):
                ratio_s[w, c] = shares[w - 1] * inv
        return 0

    def finish(c, _):
        total = out_t[c, :D, :] * ratio_s[1, c]
        prob = (prob_s[0, c] * ratio_s[0, c]).astype(jnp.bfloat16)
        out = (total + dot(v_t[0, :D, :], prob)).astype(jnp.bfloat16)
        attn_t[c] = out
        delta_s[c] = jnp.sum(
            out.astype(jnp.float32) * do_t[c].astype(jnp.float32), axis=0, keepdims=True
        )
        return 0

    def pass_back(hop, kinds=(1, 0)):
        for kind in kinds:
            total = part[hop, kind] * SCALE if kind == 0 else part[hop, kind]
            if hop > 0:
                backs[hop - 1][kind].wait_recv()
                total = total + rcv[hop - 1, kind].astype(jnp.float32)
            if hop < SPAN:
                snd[hop, kind] = total.astype(jnp.bfloat16)
                backs[hop][kind].start()
            else:
                (dk_ref, dv_ref)[kind][...] = total.astype(jnp.bfloat16).T

    def unturn(src, dst, scale):
        def one(c, _):
            for u in range(pair):
                part_ = src[c, :, u * rows : (u + 1) * rows]
                if scale is not None:
                    part_ = (part_ * scale).astype(jnp.bfloat16)
                dst[:, columns(c * pair + u)] = part_.T
            return 0

        lax.fori_loop(0, chunks, one, 0)

    def one_dv(w, c, prob):
        part[w, 1] += dot_nt(do_t[c], prob.astype(jnp.bfloat16))

    def one_dk(w, c, prob, grad):
        ds = (prob * (grad - delta_s[c])).astype(jnp.bfloat16)
        part[w, 0] += dot_nt(q_t[c], ds)
        dq_t[c] += dot(k_t[w], ds)

    def oldest_dv(half, _):
        for c in chunks_of(half):
            one_dv(0, c, prob_s[0, c] * ratio_s[0, c])
        return 0

    def oldest_dk(half, _):
        grads = [dot(kv[0, 1], do_t[c]) for c in chunks_of(half)]
        for c, grad in zip(chunks_of(half), grads):
            one_dk(0, c, prob_s[0, c] * ratio_s[0, c], grad)
        return 0

    halos[2][0].wait_recv()
    lax.fori_loop(0, 2, oldest_scores, 0)
    lax.fori_loop(0, 2, oldest_dv, 0)
    pass_back(0, (1,))
    halos[2][1].wait_recv()
    turn_kv(0)
    lax.fori_loop(0, chunks, finish, 0)
    lax.fori_loop(0, 2, oldest_dk, 0)
    pass_back(0, (0,))

    def backward(step, _):
        w, half = step // 2, lax.rem(step, 2)
        grads = [dot(kv[w, 1], do_t[c]) for c in chunks_of(half)]
        for c, grad in zip(chunks_of(half), grads):
            prob = prob_s[w, c] * ratio_s[w, c]
            one_dv(w, c, prob)
            one_dk(w, c, prob, grad)

        for hop in range(1, SPAN):

            @pl.when(step == 2 * hop + 1)
            def _(hop=hop):
                if hop == 1:
                    unturn(attn_t, attn_ref, None)
                pass_back(hop)

        return 0

    lax.fori_loop(2, 2 * WIN, backward, 0)
    unturn(dq_t, dq_ref, SCALE)
    pass_back(SPAN)

    for group in sends + halos + backs:
        for copy in group:
            copy.wait_send()


def settle(*refs):
    n = len(refs) // 2
    copies = [
        pltpu.make_async_copy(refs[i], refs[n + i], refs[-1].at[i]) for i in range(n)
    ]
    for copy in copies:
        copy.start()
    for copy in copies:
        copy.wait()


def per_device(n_seq, n_kvh, query_in, key_in, value_in, grad_out, doc_lengths):
    rows, cols = grad_out.shape
    chunks, wide = cols // (D * PAIR), PAIR * rows
    bf16, f32 = jnp.bfloat16, jnp.float32
    vmem = pl.BlockSpec(memory_space=pltpu.VMEM)
    hbm = pl.BlockSpec(memory_space=pltpu.HBM)
    dma = pltpu.SemaphoreType.DMA
    shapes = (
        jax.ShapeDtypeStruct((rows, cols), bf16),
        jax.ShapeDtypeStruct((rows, cols), bf16),
        jax.ShapeDtypeStruct((rows, D), bf16),
        jax.ShapeDtypeStruct((rows, D), bf16),
    )
    results = pl.pallas_call(
        functools.partial(kernel, n_seq, n_kvh),
        out_shape=tuple(pltpu.VMEM(shape.shape, shape.dtype) for shape in shapes),
        in_specs=[vmem, hbm, hbm, hbm, hbm],
        out_specs=(vmem, vmem, vmem, vmem),
        scratch_shapes=[
            pltpu.VMEM((rows, cols), bf16),
            pltpu.VMEM((rows, cols), bf16),
            pltpu.VMEM((chunks, D, wide), bf16),
            pltpu.VMEM((chunks, D, wide), bf16),
            pltpu.VMEM((WIN, 2, rows, D), bf16),
            pltpu.VMEM((WIN, D, rows), bf16),
            pltpu.VMEM((WIN, D + ONES, rows), bf16),
            pltpu.VMEM((WIN, rows, rows), f32),
            pltpu.VMEM((WIN, chunks, rows, wide), f32),
            pltpu.VMEM((WIN + 1, chunks, 1, wide), f32),
            pltpu.VMEM((chunks, D + ONES, wide), f32),
            pltpu.VMEM((chunks, D, wide), bf16),
            pltpu.VMEM((chunks, D, wide), f32),
            pltpu.VMEM((WIN, chunks, 1, wide), f32),
            pltpu.VMEM((chunks, 1, wide), f32),
            pltpu.VMEM((WIN, 2, D, rows), f32),
            pltpu.VMEM((SPAN, 2, D, rows), bf16),
            pltpu.VMEM((SPAN, 2, D, rows), bf16),
            dma((4,)),
            dma((4, n_kvh - 1)),
            dma((4, n_kvh - 1)),
            dma((SPAN, 2)),
            dma((SPAN, 2)),
            dma((SPAN, 2)),
            dma((SPAN, 2)),
        ],
        compiler_params=pltpu.CompilerParams(
            collective_id=0, has_side_effects=True, vmem_limit_bytes=48 * 1024 * 1024
        ),
    )(
        *(
            pltpu.with_memory_space_constraint(operand, pltpu.HBM)
            for operand in (doc_lengths.reshape(1, -1), query_in, key_in, value_in, grad_out)
        )
    )
    return pl.pallas_call(
        settle,
        out_shape=shapes,
        in_specs=[vmem] * len(shapes),
        out_specs=(hbm,) * len(shapes),
        scratch_shapes=[dma((len(shapes),))],
    )(*(pltpu.with_memory_space_constraint(result, pltpu.VMEM) for result in results))


def solution(mesh):
    placed = (
        P(("seq", "kvh"), None),
        P(("seq", "kvh"), None),
        P(("seq", "kvh"), None),
        P("seq", "kvh"),
        P(),
    )
    return jax.shard_map(
        functools.partial(per_device, mesh.shape["seq"], mesh.shape["kvh"]),
        mesh=mesh,
        in_specs=placed,
        out_specs=(P("seq", "kvh"), P("seq", "kvh"), P("seq", "kvh"), P("seq", "kvh")),
        check_vma=False,
    )
```
